32 devices in a mesh: dp: 2 (over core), fsdp: 16 (over z, y, x).
Axes of the slice: x: 2, y: 2, z: 4, core: 2. Of those that a mesh axis runs over, the one named last changes fastest.
Arguments:
- inputs: bfloat16 [32, 512, 768], P(('dp', 'fsdp')), may hold values from -6 to 6
- segments: int32 [32, 512], P(('dp', 'fsdp')), may hold values from 0 to 255, as said below
- w_q: bfloat16 [768, 768], P(('dp', 'fsdp')), may hold values from -0.21875 to 0.21875
- b_q: bfloat16 [768], P(('dp', 'fsdp')), may hold values from -1.5 to 1.5
- w_k: bfloat16 [768, 768], P(('dp', 'fsdp')), may hold values from -0.21875 to 0.21875
- w_v: bfloat16 [768, 768], P(('dp', 'fsdp')), may hold values from -0.21875 to 0.21875
- b_v: bfloat16 [768], P(('dp', 'fsdp')), may hold values from -1.5 to 1.5
- w_o: bfloat16 [768, 768], P(('dp', 'fsdp')), may hold values from -0.4375 to 0.4375
- b_o: bfloat16 [768], P(('dp', 'fsdp')), may hold values from -1.5 to 1.5
- ln1_gain: bfloat16 [768], P(('dp', 'fsdp')), may hold values from 0.5 to 1.5
- ln1_bias: bfloat16 [768], P(('dp', 'fsdp')), may hold values from -1.5 to 1.5
- w_up: bfloat16 [768, 3072], P(('dp', 'fsdp')), may hold values from -0.21875 to 0.21875
- b_up: bfloat16 [3072], P(('dp', 'fsdp')), may hold values from -1.5 to 1.5
- w_down: bfloat16 [3072, 768], P(('dp', 'fsdp')), may hold values from -0.15625 to 0.15625
- b_down: bfloat16 [768], P(('dp', 'fsdp')), may hold values from -1.5 to 1.5
- ln2_gain: bfloat16 [768], P(('dp', 'fsdp')), may hold values from 0.5 to 1.5
- ln2_bias: bfloat16 [768], P(('dp', 'fsdp')), may hold values from -1.5 to 1.5
- grad_out: bfloat16 [32, 256, 768], P(('dp', 'fsdp')), may hold values from -6 to 6
Outputs:
- output: bfloat16 [32, 256, 768], P(('dp', 'fsdp'))
- grad_inputs: float32 [32, 512, 768], P(('dp', 'fsdp'))
- grad_w_q: float32 [768, 768], P(('dp', 'fsdp'))
- grad_b_q: float32 [768], P(('dp', 'fsdp'))
- grad_w_k: float32 [768, 768], P(('dp', 'fsdp'))
- grad_w_v: float32 [768, 768], P(('dp', 'fsdp'))
- grad_b_v: float32 [768], P(('dp', 'fsdp'))
- grad_w_o: float32 [768, 768], P(('dp', 'fsdp'))
- grad_b_o: float32 [768], P(('dp', 'fsdp'))
- grad_ln1_gain: float32 [768], P(('dp', 'fsdp'))
- grad_ln1_bias: float32 [768], P(('dp', 'fsdp'))
- grad_w_up: float32 [768, 3072], P(('dp', 'fsdp'))
- grad_b_up: float32 [3072], P(('dp', 'fsdp'))
- grad_w_down: float32 [3072, 768], P(('dp', 'fsdp'))
- grad_b_down: float32 [768], P(('dp', 'fsdp'))
- grad_ln2_gain: float32 [768], P(('dp', 'fsdp'))
- grad_ln2_bias: float32 [768], P(('dp', 'fsdp'))
The draws below stay inside these ranges and needn't reach their ends.
Inputs may be any that keep to these rules, and one draw needn't show every extreme that they name: `segments`: within a row the numbers start at 0 and never fall; each document begins at an even position.
All inputs are finite; a program needn't handle non-finite values.
Results may differ from the reference program's by a relative error of at most 0.014.
Values may be sent and summed in bfloat16 or wider, within the bound.
No kernel may reach another device: no remote copies, remote signals or barrier semaphores. Data moves between devices by JAX's collectives and lax.ppermute only.
A program may use at most 128 MiB of HBM per device.

```python
import math
import jax
import jax.numpy as jnp
from jax import lax

HEAD_DIM = 64
D = 768
FF = 3072
SEQ = 512
ROWS = 32


def draw_segments(key, part):
    key = jax.random.fold_in(key, 11)
    start_key, row_key = jax.random.split(key)
    starts = (jax.random.randint(start_key, (ROWS, SEQ // 2), 0, 24) == 0).astype(jnp.int32)
    chosen = jax.random.randint(row_key, (), 0, ROWS)
    every_row = (jnp.arange(ROWS, dtype=jnp.int32) == chosen).astype(jnp.int32)[:, None]
    starts = jnp.maximum(starts, every_row)
    starts = starts.at[:, 0].set(1)
    doc_ids = jnp.cumsum(starts, axis=1) - 1
    return jnp.repeat(doc_ids, 2, axis=1).astype(jnp.int32)


def raised(array, rng, source, target, blocks, factor):
    def block_of(axis_at):
        return (jnp.arange(array.shape[axis_at]) // (array.shape[axis_at] // blocks)).reshape((-1,) + (1,) * (array.ndim - 1 - axis_at))

    one_side = jax.random.permutation(rng, blocks)[block_of(target)]
    other_side = (block_of(target) + blocks // 2) % blocks
    return jnp.where((block_of(source) == one_side) | (block_of(source) == other_side), factor * array, array)


def levels(key, shape, cuts, least, top_value):
    gain, own = 1.0, jax.random.fold_in(key, 6)
    for axis_at, blocks in cuts:
        draws = jnp.exp(jax.random.uniform(jax.random.fold_in(own, axis_at), (blocks,), jnp.float32, least / len(cuts), top_value / len(cuts)))
        gain = gain * jnp.repeat(draws, shape[axis_at] // blocks).reshape([-1 if axis == axis_at else 1 for axis in range(len(shape))])
    return gain


def gaussian(rng, shape, scale, bound, pieces=(), held_as=jnp.bfloat16):
    drawn = scale * jax.random.normal(rng, shape, jnp.float32)
    if pieces:
        drawn = drawn * levels(rng, shape, pieces, -0.22, 0.18)
    return jnp.clip(drawn, -bound, bound).astype(held_as)


def heavy_noise(key, shape, scale, bound, cuts, heavy, kind=jnp.bfloat16):
    array = scale * jax.random.normal(key, shape, jnp.float32)
    if cuts:
        array = array * levels(key, shape, cuts, -0.22, 0.18)
    return jnp.clip(raised(array, jax.random.fold_in(key, 3), *heavy), -bound, bound).astype(kind)


def setup_inputs(seed: int = 0) -> dict:
    arg_keys = jax.random.split(jax.random.key(seed), 19)
    inputs = heavy_noise(arg_keys[0], (ROWS, SEQ, D), 1.0, 6.0, ((0, 32),), (0, 2, 32, 2.75))
    segments = draw_segments(jax.random.fold_in(arg_keys[18], 71), 0)
    w_q = gaussian(arg_keys[2], (D, D), D ** -0.5, 0.21875, ((0, 32),))
    b_q = gaussian(arg_keys[3], (D,), 0.3, 1.5, ((0, 32),))
    w_k = gaussian(arg_keys[4], (D, D), D ** -0.5, 0.21875, ((0, 32),))
    w_v = gaussian(arg_keys[5], (D, D), D ** -0.5, 0.21875, ((0, 32),))
    b_v = gaussian(arg_keys[6], (D,), 0.3, 1.5, ((0, 32),))
    w_o = gaussian(arg_keys[7], (D, D), (D // 4) ** -0.5, 0.4375, ((0, 32),))
    b_o = gaussian(arg_keys[8], (D,), 0.3, 1.5, ((0, 32),))
    ln1_gain = jnp.clip(1.0 + 0.1 * jax.random.normal(arg_keys[9], (D,), jnp.float32), 0.5, 1.5).astype(jnp.bfloat16)
    ln1_bias = gaussian(arg_keys[10], (D,), 0.3, 1.5, ((0, 32),))
    w_up = gaussian(arg_keys[11], (D, FF), D ** -0.5, 0.21875, ((0, 32),))
    b_up = gaussian(arg_keys[12], (FF,), 0.3, 1.5, ((0, 32),))
    w_down = gaussian(arg_keys[13], (FF, D), (FF // 2) ** -0.5, 0.15625, ((0, 32),))
    b_down = gaussian(arg_keys[14], (D,), 0.3, 1.5, ((0, 32),))
    ln2_gain = jnp.clip(1.0 + 0.1 * jax.random.normal(arg_keys[15], (D,), jnp.float32), 0.5, 1.5).astype(jnp.bfloat16)
    ln2_bias = gaussian(arg_keys[16], (D,), 0.3, 1.5, ((0, 32),))
    grad_out = heavy_noise(arg_keys[17], (ROWS, SEQ // 2, D), 1.0, 6.0, ((0, 32),), (0, 2, 32, 2.75))
    return {"inputs": inputs, "segments": segments, "w_q": w_q, "b_q": b_q, "w_k": w_k, "w_v": w_v, "b_v": b_v, "w_o": w_o, "b_o": b_o, "ln1_gain": ln1_gain, "ln1_bias": ln1_bias, "w_up": w_up, "b_up": b_up, "w_down": w_down, "b_down": b_down, "ln2_gain": ln2_gain, "ln2_bias": ln2_bias, "grad_out": grad_out}


@jax.custom_vjp
def low(v):
    return lax.optimization_barrier(v.astype(jnp.bfloat16)).astype(jnp.float32)

@jax.custom_vjp
def low_back(v):
    return v

def low_keep(v):
    return (low(v), None)

def low_pass(kept, grad):
    return (grad,)

def back_keep(v):
    return (v, None)

def back_low(kept, grad):
    return (low(grad),)
low.defvjp(low_keep, low_pass)
low_back.defvjp(back_keep, back_low)
EPSILON = 1e-06
HIGHEST = lax.Precision.HIGHEST

def matmul_high(left, right):
    return jnp.einsum('...d,df->...f', left, right, precision=HIGHEST)

def layer_norm(hidden):
    center = hidden - lax.optimization_barrier(jnp.mean(hidden, axis=-1, keepdims=True))
    spread = lax.optimization_barrier(jnp.mean(center * center, axis=-1, keepdims=True))
    return center * lax.rsqrt(spread + EPSILON)

def position_bias(head_count, half_length, seq_length):
    slopes = 2.0 ** (-8.0 * (jnp.arange(head_count, dtype=jnp.float32) + 1.0) / head_count)
    query_pos = 2.0 * jnp.arange(half_length, dtype=jnp.float32) + 0.5
    key_pos = jnp.arange(seq_length, dtype=jnp.float32)
    distance = jnp.abs(key_pos[None, :] - query_pos[:, None])
    return -slopes[:, None, None] * distance[None]

def forward(hidden, segments, w_q, b_q, w_k, w_v, b_v, w_o, b_o, ln1_gain, ln1_bias, w_up, b_up, w_down, b_down, ln2_gain, ln2_bias):
    row_count, seq_length, model_width = hidden.shape
    half_length = seq_length // 2
    head_count = model_width // HEAD_DIM
    pooled = (hidden[:, 0::2] + hidden[:, 1::2]) * 0.5
    query_rows = low(low_back(matmul_high(low(pooled), w_q) + b_q)).reshape(row_count, half_length, head_count, HEAD_DIM)
    key_rows = low(low_back(matmul_high(hidden, w_k))).reshape(row_count, seq_length, head_count, HEAD_DIM)
    value_rows = low(low_back(matmul_high(hidden, w_v) + b_v)).reshape(row_count, seq_length, head_count, HEAD_DIM)
    scores = jnp.einsum('rphe,rlhe->rhpl', query_rows, key_rows, precision=HIGHEST) * 0.125
    scores = scores + position_bias(head_count, half_length, seq_length)[None]
    same_doc = segments[:, 0::2][:, None, :, None] == segments[:, None, None, :]
    scores = low_back(jnp.where(same_doc, scores, -1000000000.0))
    log_total = jax.scipy.special.logsumexp(scores, axis=-1, keepdims=True)
    probs = low(jnp.exp(scores - log_total))
    mixed = jnp.einsum('rhpl,rlhe->rphe', probs, value_rows, precision=HIGHEST)
    mixed = low(low_back(mixed)).reshape(row_count, half_length, model_width)
    branch = low_back(matmul_high(mixed, w_o) + b_o)
    first_out = layer_norm(pooled + branch) * ln1_gain + ln1_bias
    inner_act = low_back(matmul_high(low(first_out), w_up) + b_up)
    second_out = low_back(matmul_high(low(jax.nn.gelu(inner_act)), w_down) + b_down)
    return layer_norm(first_out + second_out) * ln2_gain + ln2_bias

def reference(inputs, segments, w_q, b_q, w_k, w_v, b_v, w_o, b_o, ln1_gain, ln1_bias, w_up, b_up, w_down, b_down, ln2_gain, ln2_bias, grad_out):
    params = tuple((weight.astype(jnp.float32) for weight in (w_q, b_q, w_k, w_v, b_v, w_o, b_o, ln1_gain, ln1_bias, w_up, b_up, w_down, b_down, ln2_gain, ln2_bias)))
    row_count, seq_length, model_width = inputs.shape
    half_length = seq_length // 2
    group = math.gcd(row_count, max(1, 4096 // seq_length))
    blocks = row_count // group
    hidden_all = inputs.astype(jnp.float32).reshape(blocks, group, seq_length, model_width)
    segment_all = segments.reshape(blocks, group, seq_length)
    upstream_all = grad_out.astype(jnp.float32).reshape(blocks, group, half_length, model_width)

    def step(running, batch_item):
        hidden, segment_block, upstream = batch_item

        def local_forward(hidden_in, *weights):
            return forward(hidden_in, segment_block, *weights)
        result, pullback = jax.vjp(local_forward, hidden, *params)
        grads = pullback(upstream)
        running = tuple((acc + new for acc, new in zip(running, grads[1:])))
        return (running, (result, grads[0]))
    zeros = tuple((jnp.zeros_like(weight) for weight in params))
    totals, (results, input_grads) = lax.scan(step, zeros, (hidden_all, segment_all, upstream_all))
    output = results.reshape(row_count, half_length, model_width).astype(jnp.bfloat16)
    grad_inputs = input_grads.reshape(row_count, seq_length, model_width)
    return (output, grad_inputs, totals[0], totals[1], totals[2], totals[3], totals[4], totals[5], totals[6], totals[7], totals[8], totals[9], totals[10], totals[11], totals[12], totals[13], totals[14])
```

```python
import functools

import jax
import jax.numpy as jnp
from jax import lax
from jax.experimental import pallas as pl
from jax.experimental.pallas import tpu as pltpu
from jax.sharding import PartitionSpec as P

HEAD_DIM = 64
LANES = 128
EPSILON = 1e-06
FAR = 1e12
AXES = ("dp", "fsdp")
BF16 = jnp.bfloat16
F32 = jnp.float32
VMEM_BYTES = 48 * 1024 * 1024


def nn_dot(left, right):
    return jnp.dot(left, right, preferred_element_type=F32)


def nt_dot(left, right):
    return lax.dot_general(left, right, (((1,), (1,)), ((), ())), preferred_element_type=F32)


def tn_dot(left, right):
    return lax.dot_general(left, right, (((0,), (0,)), ((), ())), preferred_element_type=F32)


def iota(shape, axis):
    return lax.broadcasted_iota(jnp.int32, shape, axis)


def ones_where(condition):
    return jnp.where(condition, 1.0, 0.0).astype(BF16)


def two_parts(array):
    high = array.astype(BF16)
    return high, (array - high.astype(F32)).astype(BF16)


def mean_of(array):
    return jnp.mean(array, axis=-1, keepdims=True)


def gelu_parts(value):
    scale = 0.7978845608028654
    square = value * value
    bend = jnp.tanh(scale * value * (1.0 + 0.044715 * square))
    half = 0.5 * (1.0 + bend)
    slope = half + 0.5 * value * (1.0 - bend * bend) * scale * (1.0 + 3.0 * 0.044715 * square)
    return value * half, slope


COL_BQ, COL_BV, COL_BO, COL_G1, COL_S1, COL_BD, COL_G2, COL_S2, COL_BU = 0, 1, 2, 3, 4, 5, 6, 7, 8


def up_spread(half, ff_half, per_up):
    rows = iota((half, ff_half), 0)
    cols = iota((half, ff_half), 1)
    per_row = half * per_up // ff_half
    same_chip = rows // per_row == cols // per_up
    same_place = rows % per_row == cols % per_row
    return ones_where(same_chip & same_place)


def segment_parts(act_ref, row, row_count, half_length, seq_length):
    base = row_count * (seq_length + half_length)
    seg_rows = act_ref[base : base + 16, :seq_length]
    evens = ones_where(iota((half_length, seq_length), 1) == 2 * iota((half_length, seq_length), 0))
    return seg_rows, evens


def attend_kernel(
    sizes, core_ref, slope_ref, act_own, act_other, wa, q_out, k_out, v_out, mixed_out, pooled_out,
    table_out, bup_out, dm,
):
    row_count, seq_length, half_length, width, ff_half, per_up = sizes
    half = width // 2
    core = core_ref[0]
    eye = ones_where(iota((16, LANES), 0) == iota((16, LANES), 1))
    table = nt_dot(eye, wa[:, 2 * width : 2 * width + LANES])
    table_out[...] = table
    mine = jnp.where(core == 0, table[:, :half], table[:, half:])
    spread = nn_dot(mine.astype(BF16), up_spread(half, ff_half, per_up))
    per_row = half * per_up // ff_half
    which = (iota((16, ff_half), 1) % per_up) // per_row + COL_BU
    bup = jnp.sum(jnp.where(iota((16, ff_half), 0) == which, spread, 0.0), axis=0, keepdims=True)
    bup_out[...] = jnp.broadcast_to(bup, (8, ff_half))
    pair = (iota((half_length, seq_length), 1) // 2) == iota((half_length, seq_length), 0)
    pool = jnp.where(pair, 0.5, 0.0).astype(BF16)
    lane = iota((1, LANES), 1)
    masks = [ones_where(lane < HEAD_DIM), ones_where(lane >= HEAD_DIM)]
    bias_q, bias_v = mine[COL_BQ : COL_BQ + 1], mine[COL_BV : COL_BV + 1]
    for row in range(2 * row_count):
        act = act_own if row < row_count else act_other
        local = row % row_count
        hidden = act[local * seq_length : (local + 1) * seq_length, :]
        pooled = nn_dot(pool, hidden)
        pooled_out[row] = pooled
        query = nn_dot(pooled.astype(BF16), wa[:, :half]) + bias_q
        q_out[row] = (query.astype(BF16).astype(F32) * 0.125).astype(BF16)
        k_out[row] = nn_dot(hidden, wa[:, half : 2 * half]).astype(BF16)
        v_out[row] = (nn_dot(hidden, wa[:, 2 * half : 3 * half]) + bias_v).astype(BF16)
        seg_rows, evens = segment_parts(act, local, row_count, half_length, seq_length)
        seg_query = nt_dot(evens, seg_rows)[:, local : local + 1]
        seg_key = seg_rows[local : local + 1].astype(F32)
        shape = (half_length, seq_length)
        distance = jnp.abs((iota(shape, 1) - 2 * iota(shape, 0)).astype(F32) - 0.5)
        dm[...] = jnp.where(seg_query == seg_key, distance, FAR)
        for place in range(half // LANES):
            cols = slice(place * LANES, (place + 1) * LANES)
            q_pair, k_pair, v_pair = q_out[row, :, cols], k_out[row, :, cols], v_out[row, :, cols]
            results = []
            for sub in range(2):
                slope = slope_ref[2 * place + sub]
                scores = nt_dot(q_pair * masks[sub], k_pair) - slope * dm[...]
                peak = jnp.max(scores, axis=-1, keepdims=True)
                raised = jnp.exp(scores - peak)
                total = jnp.sum(raised, axis=-1, keepdims=True)
                probs = (raised * (1.0 / total)).astype(BF16)
                results.append(nn_dot(probs, v_pair))
            mixed_out[row, :, cols] = jnp.where(lane < HEAD_DIM, results[0], results[1]).astype(BF16)


def ffn_kernel(
    sizes, pooled, mixed_own, mixed_other, wo_own, wo_other, table, bup, up, down,
    normed_out, inverse_out, low_out, active_out, bend_out, part_out, send_out,
):
    row_count, seq_length, half_length, width, ff_half, per_up = sizes
    half = width // 2
    for row in range(2 * row_count):
        rows = slice(row * half_length, (row + 1) * half_length)
        own = mixed_own[row]
        other = mixed_other[(row + row_count) % (2 * row_count)]
        parts = [nn_dot(own, wo_own[side]) + nn_dot(other, wo_other[side]) for side in range(2)]
        hidden = pooled[rows, :] + (jnp.concatenate(parts, axis=1) + table[COL_BO : COL_BO + 1, :])
        center = hidden - mean_of(hidden)
        inverse = lax.rsqrt(mean_of(center * center) + EPSILON)
        normed = center * inverse
        normed_out[rows, :] = normed
        inverse_out[rows, :] = jnp.broadcast_to(inverse, (half_length, LANES))
        first = normed * table[COL_G1 : COL_G1 + 1, :] + table[COL_S1 : COL_S1 + 1, :]
        low_out[rows, :] = first.astype(BF16)
    chunk = 256
    for start in range(0, ff_half, chunk):
        cols = slice(start, start + chunk)
        side, inside = divmod(start, width)
        inner = nn_dot(low_out[...], up[side, :, inside : inside + chunk]) + bup[0:1, cols]
        active, slope = gelu_parts(inner)
        active_out[:, cols] = active.astype(BF16)
        bend_out[:, cols] = slope
    for start in range(0, width, chunk):
        cols = slice(start, start + chunk)
        part = nn_dot(active_out[...], down[:, cols])
        part_out[:, cols] = part
        send_out[:, cols] = part.astype(BF16)


def ffn_back_kernel(
    sizes, act_own, act_other, normed_one, part_own, part_other, table, bend, up, down,
    out_out, gh2_out, gsec_out, ginner_out, gfirst_out, gsend_out, sums_out, gbup_out,
):
    row_count, seq_length, half_length, width, ff_half, per_up = sizes
    gain_two = table[COL_G2 : COL_G2 + 1, :]
    sum_gain = jnp.zeros((1, width), F32)
    sum_shift = jnp.zeros((1, width), F32)
    sum_down = jnp.zeros((1, width), F32)
    for row in range(2 * row_count):
        rows = slice(row * half_length, (row + 1) * half_length)
        swapped = (row + row_count) % (2 * row_count)
        other_rows = slice(swapped * half_length, (swapped + 1) * half_length)
        act = act_own if row < row_count else act_other
        base = row_count * seq_length + (row % row_count) * half_length
        first = normed_one[rows, :] * table[COL_G1 : COL_G1 + 1, :] + table[COL_S1 : COL_S1 + 1, :]
        second = part_own[rows, :] + part_other[other_rows, :].astype(F32) + table[COL_BD : COL_BD + 1, :]
        hidden = first + second
        center = hidden - mean_of(hidden)
        inverse = lax.rsqrt(mean_of(center * center) + EPSILON)
        normed = center * inverse
        if row < row_count:
            out_out[rows, :] = (normed * gain_two + table[COL_S2 : COL_S2 + 1, :]).astype(BF16)
        upstream = act[base : base + half_length, :].astype(F32)
        sum_gain += jnp.sum(upstream * normed, axis=0, keepdims=True)
        sum_shift += jnp.sum(upstream, axis=0, keepdims=True)
        scaled = upstream * gain_two
        grad = inverse * (scaled - mean_of(scaled) - normed * mean_of(scaled * normed))
        gh2_out[rows, :] = grad
        low = grad.astype(BF16)
        gsec_out[rows, :] = low
        sum_down += jnp.sum(low.astype(F32), axis=0, keepdims=True)
    sums_out[...] = jnp.concatenate([sum_gain, sum_shift, sum_down, jnp.zeros((5, width), F32)], axis=0)
    chunk = 256
    for start in range(0, ff_half, chunk):
        cols = slice(start, start + chunk)
        grad = (nt_dot(gsec_out[...], down[cols, :]) * bend[:, cols]).astype(BF16)
        ginner_out[:, cols] = grad
        total = jnp.sum(grad.astype(F32), axis=0, keepdims=True)
        gbup_out[:, cols] = jnp.broadcast_to(total, (8, chunk))
    for start in range(0, width, chunk):
        cols = slice(start, start + chunk)
        part = nt_dot(ginner_out[:, :width], up[0, cols, :]) + nt_dot(ginner_out[:, width:], up[1, cols, :])
        gfirst_out[:, cols] = part
        gsend_out[:, cols] = part.astype(BF16)


def ffn_weight_kernel(low, active, gsec, ginner, gup_out, gdown_out):
    width = low.shape[1]
    chunk = 256
    for start in range(0, active.shape[1], chunk):
        gdown_out[start : start + chunk, :] = tn_dot(active[:, start : start + chunk], gsec[...])
    for side in range(2):
        for start in range(0, width, chunk):
            gup_out[side, start : start + chunk, :] = tn_dot(
                low[:, start : start + chunk], ginner[:, side * width : (side + 1) * width]
            )


def attend_back_kernel(
    sizes, core_ref, slope_ref, act_own, act_other, normed_one, inverse_one, gh2, gfirst_own, gfirst_other,
    table, mixed_own, wo_own, query, key, value,
    gh1_out, gq_out, gk_out, gv_out, gwo_out, sums_out, heads_out, dm, gbranch, gmixed,
):
    row_count, seq_length, half_length, width, ff_half, per_up = sizes
    half = width // 2
    gain_one = table[COL_G1 : COL_G1 + 1, :]
    zero = jnp.zeros((1, width), F32)
    sum_gain, sum_shift, sum_out = zero, zero, zero
    for row in range(2 * row_count):
        rows = slice(row * half_length, (row + 1) * half_length)
        swapped = (row + row_count) % (2 * row_count)
        other_rows = slice(swapped * half_length, (swapped + 1) * half_length)
        grad = gh2[rows, :] + (gfirst_own[rows, :] + gfirst_other[other_rows, :].astype(F32))
        normed = normed_one[rows, :]
        sum_gain += jnp.sum(grad * normed, axis=0, keepdims=True)
        sum_shift += jnp.sum(grad, axis=0, keepdims=True)
        scaled = grad * gain_one
        inverse = inverse_one[rows, 0:1]
        grad = inverse * (scaled - mean_of(scaled) - normed * mean_of(scaled * normed))
        gh1_out[rows, :] = grad
        low = grad.astype(BF16)
        gbranch[rows, :] = low
        sum_out += jnp.sum(low.astype(F32), axis=0, keepdims=True)
    sums_out[...] = jnp.concatenate([sum_gain, sum_shift, sum_out, jnp.zeros((5, width), F32)], axis=0)
    gmixed[...] = (
        nt_dot(gbranch[:, :half], wo_own[0]) + nt_dot(gbranch[:, half:], wo_own[1])
    ).astype(BF16)
    total = jnp.zeros((half, width), F32)
    for row in range(2 * row_count):
        total += tn_dot(mixed_own[row], gbranch[row * half_length : (row + 1) * half_length, :])
    gwo_out[...] = total
    lane = iota((1, LANES), 1)
    masks = [ones_where(lane < HEAD_DIM), ones_where(lane >= HEAD_DIM)]
    sums_q = jnp.zeros((1, half), F32)
    sums_v = jnp.zeros((1, half), F32)
    shape = (seq_length, half_length)
    for row in range(2 * row_count):
        act = act_own if row < row_count else act_other
        local = row % row_count
        base = row_count * (seq_length + half_length)
        seg_rows = act[base : base + 16, :seq_length]
        eye = ones_where(iota((seq_length, seq_length), 0) == iota((seq_length, seq_length), 1))
        evens = ones_where(iota((half_length, seq_length), 1) == 2 * iota((half_length, seq_length), 0))
        seg_key = nt_dot(eye, seg_rows)[:, local : local + 1]
        seg_query = nt_dot(seg_rows, evens)[local : local + 1, :]
        distance = jnp.abs((iota(shape, 0) - 2 * iota(shape, 1)).astype(F32) - 0.5)
        dm[...] = jnp.where(seg_query == seg_key, distance, FAR)
        for place in range(half // LANES):
            cols = slice(place * LANES, (place + 1) * LANES)
            q_pair, k_pair, v_pair = query[row, :, cols], key[row, :, cols], value[row, :, cols]
            g_pair = gmixed[row * half_length : (row + 1) * half_length, cols]
            found = []
            for sub in range(2):
                slope = slope_ref[2 * place + sub]
                scores = nt_dot(k_pair, q_pair * masks[sub]) - slope * dm[...]
                peak = jnp.max(scores, axis=0, keepdims=True)
                raised = jnp.exp(scores - peak)
                exact = raised * (1.0 / jnp.sum(raised, axis=0, keepdims=True))
                gprobs = nt_dot(v_pair, g_pair * masks[sub])
                mean = jnp.sum(exact * gprobs, axis=0, keepdims=True)
                gscores = (exact * (gprobs - mean)).astype(BF16)
                found.append(
                    (
                        nn_dot(exact.astype(BF16), g_pair),
                        nn_dot(gscores, q_pair),
                        tn_dot(gscores, k_pair) * 0.125,
                    )
                )
            gvalue, gkey, gquery = (
                jnp.where(lane < HEAD_DIM, a, b).astype(BF16) for a, b in zip(found[0], found[1])
            )
            gv_out[row, :, cols] = gvalue
            gk_out[row, :, cols] = gkey
            gq_out[row, :, cols] = gquery
        sums_q += jnp.sum(gq_out[row].astype(F32), axis=0, keepdims=True)
        sums_v += jnp.sum(gv_out[row].astype(F32), axis=0, keepdims=True)
    heads_out[...] = jnp.concatenate([sums_q, sums_v, jnp.zeros((6, half), F32)], axis=0)


def attend_weight_kernel(
    sizes, core_ref, act_own, act_other, pooled, gq, gk, gv, gwo, sums_one, sums_two, heads, gbup, grads_out
):
    row_count, seq_length, half_length, width, ff_half, per_up = sizes
    half = width // 2
    core = core_ref[0]
    pooled_low = pooled[...].astype(BF16)
    gq_all = jnp.concatenate([gq[row] for row in range(2 * row_count)], axis=0)
    grads_out[:, :half] = tn_dot(pooled_low, gq_all)
    for index, grad in ((1, gk), (2, gv)):
        total = None
        for row in range(2 * row_count):
            act = act_own if row < row_count else act_other
            local = row % row_count
            hidden = act[local * seq_length : (local + 1) * seq_length, :]
            term = tn_dot(hidden, grad[row])
            total = term if total is None else total + term
        grads_out[:, index * half : (index + 1) * half] = total
    grads_out[:half, 3 * half : 4 * half] = gwo[:, :half]
    grads_out[half:, 3 * half : 4 * half] = gwo[:, half:]
    one = jnp.where(core == 0, sums_one[:, :half], sums_one[:, half:])
    two = jnp.where(core == 0, sums_two[:, :half], sums_two[:, half:])
    per_row = half * per_up // ff_half
    which = (iota((8, ff_half), 1) % per_up) // per_row
    spread = up_spread(half, ff_half, per_up)
    picked = jnp.where(iota((8, ff_half), 0) == which, gbup[...], 0.0)
    high, low = two_parts(picked)
    ups = nt_dot(high, spread) + nt_dot(low, spread)
    stacked = jnp.concatenate(
        [
            heads[0:2], one[2:3], one[0:2], two[2:3], two[0:2], ups,
            jnp.zeros((LANES - 16, half), F32),
        ],
        axis=0,
    )
    grads_out[:half, 4 * half : 4 * half + LANES] = stacked.T
    grads_out[half:, 4 * half : 4 * half + LANES] = jnp.zeros((half, LANES), F32)


def input_grad(sizes, row, gq, gk, gv, wa, extra):
    row_count, seq_length, half_length, width, ff_half, per_up = sizes
    half = width // 2
    grad = nt_dot(gk[row], wa[:, half : 2 * half]) + nt_dot(gv[row], wa[:, 2 * half : 3 * half])
    pooled = nt_dot(gq[row], wa[:, :half])
    if extra is not None:
        pooled = pooled + extra
    high, low = two_parts(pooled)
    shape = (seq_length, half_length)
    split = jnp.where(iota(shape, 0) // 2 == iota(shape, 1), 0.5, 0.0).astype(BF16)
    return grad + (nn_dot(split, high) + nn_dot(split, low))


def other_inputs_kernel(sizes, gq, gk, gv, wa, send_out):
    row_count, seq_length = sizes[0], sizes[1]
    for local in range(row_count):
        grad = input_grad(sizes, row_count + local, gq, gk, gv, wa, None)
        send_out[local * seq_length : (local + 1) * seq_length, :] = grad.astype(BF16)


def own_inputs_kernel(sizes, gq, gk, gv, wa, gh1, received, grad_out):
    row_count, seq_length, half_length = sizes[0], sizes[1], sizes[2]
    for local in range(row_count):
        extra = gh1[local * half_length : (local + 1) * half_length, :]
        grad = input_grad(sizes, local, gq, gk, gv, wa, extra)
        rows = slice(local * seq_length, (local + 1) * seq_length)
        grad_out[rows, :] = grad + received[rows, :].astype(F32)


def run_kernel(kernel, outs, operands, scratch=(), scalars=0, flops=0):
    specs = [pl.BlockSpec(memory_space=pltpu.SMEM)] * scalars
    specs += [pl.BlockSpec(memory_space=pltpu.VMEM)] * (len(operands) - scalars)
    moved = sum(a.size * a.dtype.itemsize for a in list(operands) + list(outs))
    return pl.pallas_call(
        kernel,
        out_shape=tuple(outs),
        in_specs=specs,
        out_specs=tuple(pl.BlockSpec(memory_space=pltpu.VMEM) for _ in outs),
        scratch_shapes=list(scratch),
        compiler_params=pltpu.CompilerParams(vmem_limit_bytes=VMEM_BYTES),
        cost_estimate=pl.CostEstimate(flops=int(flops), bytes_accessed=moved, transcendentals=0),
    )(*operands)


def shape_of(shape, dtype):
    return jax.ShapeDtypeStruct(shape, dtype)


class Chips:
    def __init__(self):
        index = lax.axis_index("fsdp")
        self.z, self.y, self.x = index // 4, (index // 2) % 2, index % 2

    def shift(self, array, step):
        pairs = [(i, (i + 4 * step) % 16) for i in range(16)]
        return lax.ppermute(array, "fsdp", pairs)

    def swap(self, array, bit):
        return lax.ppermute(array, "fsdp", [(i, i ^ bit) for i in range(16)])

    def ordered(self, bit, own, received):
        buffer = jnp.zeros((2,) + own.shape, own.dtype)
        buffer = lax.dynamic_update_index_in_dim(buffer, own, bit, 0)
        return lax.dynamic_update_index_in_dim(buffer, received, 1 - bit, 0)

    def gather(self, pack):
        around = [self.shift(pack, step) for step in (1, 2, 3)]
        column = jnp.zeros((2, 4) + pack.shape[1:], pack.dtype)
        column = lax.dynamic_update_index_in_dim(column, pack, self.z, 1)
        for step, block in zip((1, 2, 3), around):
            column = lax.dynamic_update_index_in_dim(column, block, (self.z - step) % 4, 1)
        one, two = column[0], column[1]
        one_x, two_y = self.swap(one, 1), self.swap(two, 2)
        one_row = self.ordered(self.x, one, one_x)
        two_row = self.ordered(self.y, two, two_y)
        one_y, two_x = self.swap(one_row, 2), self.swap(two_row, 1)
        one_all = self.ordered(self.y, one_row, one_y)
        two_all = jnp.swapaxes(self.ordered(self.x, two_row, two_x), 0, 1)
        return [jnp.transpose(a, (2, 0, 1) + tuple(range(3, a.ndim))) for a in (one_all, two_all)]

    def scatter(self, one, two):
        pick = lax.dynamic_index_in_dim
        one_x = self.swap(pick(one, 1 - self.x, 2, False).astype(BF16), 1)
        two_y = self.swap(pick(two, 1 - self.y, 1, False).astype(BF16), 2)
        one = pick(one, self.x, 2, False) + one_x.astype(F32)
        two = pick(two, self.y, 1, False) + two_y.astype(F32)
        one_y = self.swap(pick(one, 1 - self.y, 1, False).astype(BF16), 2)
        two_x = self.swap(pick(two, 1 - self.x, 1, False).astype(BF16), 1)
        one = pick(one, self.y, 1, False) + one_y.astype(F32)
        two = pick(two, self.x, 1, False) + two_x.astype(F32)
        both = jnp.stack([one, two], axis=1)
        total = pick(both, self.z, 0, False)
        for step in (1, 2, 3):
            block = pick(both, (self.z + step) % 4, 0, False).astype(BF16)
            total = total + self.shift(block, step).astype(F32)
        return total


def half_columns(array, which):
    size = array.shape[1] // 2
    return lax.dynamic_slice_in_dim(array, which * size, size, axis=1)


def halves(array):
    size = array.shape[1] // 2
    return [array[:, :size], array[:, size:]]


def gather_by_chips(core, swap_cores, weights):
    w_q, w_k, w_v, w_o, biases, w_up, w_down = weights
    chips = Chips()
    per_row, width = w_q.shape
    half = width // 2

    def columns_for(which):
        parts = [half_columns(w, which) for w in (w_q, w_k, w_v)]
        return jnp.concatenate(parts + [biases, half_columns(w_up, which)], axis=1)

    received = swap_cores(columns_for(1 - core))
    both = chips.ordered(core, columns_for(core), received)
    o_halves = jnp.stack(halves(w_o), axis=0)
    pack = jnp.concatenate([both[:, :, : 3 * half], o_halves, both[:, :, 3 * half : 3 * half + LANES]], axis=2)
    wa = jnp.stack([a.reshape(half, -1) for a in chips.gather(pack)], axis=0)
    wo_own = wa[:, :, 3 * half : 4 * half]
    up_parts = both[:, :, 3 * half + LANES :]
    down_rows = w_down.shape[0] // 2
    packs = []
    for part in range(2):
        up_part = up_parts[:, :, part * width : (part + 1) * width].reshape(2 * per_row, width)
        packs.append(jnp.concatenate([up_part, w_down[part * down_rows : (part + 1) * down_rows]], axis=0))
    gathered = chips.gather(jnp.stack(packs, axis=0))
    ups = [a[..., : 2 * per_row, :].reshape(16, 2, per_row, width) for a in gathered]
    up = jnp.stack([jnp.swapaxes(a, 0, 1).reshape(width, width) for a in ups], axis=0)
    downs = [a[..., 2 * per_row :, :].reshape(16, down_rows, width) for a in gathered]
    return wa.reshape(width, -1), wo_own, up, jnp.stack(downs, axis=1).reshape(-1, width)


def gather_flat(core, weights):
    w_q, w_k, w_v, w_o, biases, w_up, w_down = (lax.all_gather(w, AXES, axis=0, tiled=True) for w in weights)
    width = w_q.shape[0]
    half = width // 2
    wo_own = jnp.stack(halves(lax.dynamic_slice_in_dim(w_o, core * half, half)), axis=0)
    columns = [half_columns(w, core) for w in (w_q, w_k, w_v)]
    wa = jnp.concatenate(columns + [wo_own.reshape(width, half), biases], axis=1)
    up = jnp.stack(halves(half_columns(w_up, core)), axis=0)
    ff_half = w_down.shape[0] // 2
    return wa, wo_own, up, lax.dynamic_slice_in_dim(w_down, core * ff_half, ff_half)


def scatter_ffn(gup, gdown, per_row):
    width = gup.shape[1]
    grid = (4, 2, 2)
    gup = jnp.moveaxis(gup.reshape((2, 2) + grid + (per_row, width)), 1, 4)
    gup = gup.reshape((2,) + grid + (2 * per_row, width))
    gdown = gdown.reshape(grid + (2, -1, width))
    parts = [jnp.concatenate([gup[part], gdown[:, :, :, part]], axis=3) for part in range(2)]
    return Chips().scatter(parts[0], parts[1])


def scatter_rows(array):
    return lax.psum_scatter(array, AXES, scatter_dimension=0, tiled=True)


def placed(array, core, axis):
    shape = list(array.shape)
    shape[axis] *= 2
    return lax.dynamic_update_slice_in_dim(jnp.zeros(shape, array.dtype), array, core * array.shape[axis], axis)


def scatter_ffn_flat(core, gup, gdown):
    up = placed(jnp.concatenate([gup[0], gup[1]], axis=1), core, 1)
    return scatter_rows(up), scatter_rows(placed(gdown, core, 0))


def scatter_attention_flat(core, grads):
    width = grads.shape[0]
    half = width // 2
    found = [scatter_rows(placed(grads[:, i * half : (i + 1) * half], core, 1)) for i in range(3)]
    wo = jnp.concatenate([grads[:half, 3 * half : 4 * half], grads[half:, 3 * half : 4 * half]], axis=1)
    found.append(scatter_rows(placed(wo, core, 0)))
    found.append(scatter_rows(placed(grads[:half, 4 * half :], core, 0)))
    return found


def joined(core, swap_cores, array):
    send = lax.dynamic_index_in_dim(array, 1 - core, 0, False)
    keep = lax.dynamic_index_in_dim(array, core, 0, False)
    received = swap_cores(send)
    return jnp.where(core == 0, jnp.concatenate([keep, received], -1), jnp.concatenate([received, keep], -1))


def join_ffn(core, swap_cores, total, per_row):
    width = total.shape[-1]
    up = total[:, : 2 * per_row].reshape(2, 2, per_row, width)
    up = jnp.concatenate([up[0], up[1]], axis=-1)
    return joined(core, swap_cores, up), total[:, 2 * per_row :].reshape(-1, width)


def join_attention(core, swap_cores, total):
    per_row = total.shape[1]
    half = (total.shape[2] - LANES) // 4
    attn = joined(core, swap_cores, total[:, :, : 3 * half].reshape(2, per_row, 3, half))
    wo = jnp.concatenate([total[0, :, 3 * half : 4 * half], total[1, :, 3 * half : 4 * half]], axis=-1)
    return attn[:, 0], attn[:, 1], attn[:, 2], wo, total[0, :, 4 * half :]


def body(mesh_shape, *args):
    (
        inputs, segments, w_q, b_q, w_k, w_v, b_v, w_o, b_o, ln1_gain, ln1_bias, w_up, b_up, w_down,
        b_down, ln2_gain, ln2_bias, grad_out,
    ) = args
    dp_size, fsdp_size = mesh_shape
    row_count, seq_length, width = inputs.shape
    half_length = seq_length // 2
    half = width // 2
    per_row, ff = w_up.shape
    ff_half = ff // 2
    per_up = w_down.shape[0]
    ratio = per_up // per_row
    sizes = (row_count, seq_length, half_length, width, ff_half, per_up)
    tokens = 2 * row_count * half_length
    core = lax.axis_index("dp") % 2
    core_at = core.reshape(1).astype(jnp.int32)
    heads = width // HEAD_DIM
    slopes = 2.0 ** (-8.0 * (jnp.arange(heads, dtype=F32) + 1.0) / heads)
    slopes = lax.dynamic_slice_in_dim(slopes, core * (heads // 2), heads // 2)
    swap_pairs = [(i, i ^ 1) for i in range(dp_size)]

    def swap_cores(array):
        return lax.ppermute(array, "dp", swap_pairs)

    seg_rows = jnp.pad(segments.astype(BF16), ((0, 16 - row_count), (0, width - seq_length)))
    act_own = jnp.concatenate(
        [inputs.reshape(-1, width), grad_out.reshape(-1, width), seg_rows], axis=0
    )

    biases = jnp.stack([b_q, b_v, b_o, ln1_gain, ln1_bias, b_down, ln2_gain, ln2_bias], axis=0)
    biases = jnp.concatenate([biases, b_up.reshape(ratio, per_row)], axis=0)
    biases = jnp.pad(biases, ((0, LANES - 8 - ratio), (0, 0))).T

    act_other = swap_cores(act_own)
    weights = (w_q, w_k, w_v, w_o, biases, w_up, w_down)
    if (dp_size, fsdp_size) == (2, 16):
        wa, wo_own, up, down = gather_by_chips(core, swap_cores, weights)
    else:
        wa, wo_own, up, down = gather_flat(core, weights)

    rows2 = 2 * row_count
    q_rows, k_rows, v_rows, mixed, pooled, table, bup = run_kernel(
        functools.partial(attend_kernel, sizes),
        [
            shape_of((rows2, half_length, half), BF16),
            shape_of((rows2, seq_length, half), BF16),
            shape_of((rows2, seq_length, half), BF16),
            shape_of((rows2, half_length, half), BF16),
            shape_of((rows2, half_length, width), F32),
            shape_of((16, width), F32),
            shape_of((8, ff_half), F32),
        ],
        [core_at, slopes, act_own, act_other, wa],
        [pltpu.VMEM((half_length, seq_length), F32)],
        scalars=2,
        flops=8e9,
    )
    wo_other = swap_cores(wo_own)
    mixed_other = swap_cores(mixed)
    pooled = pooled.reshape(tokens, width)
    normed_one, inverse_one, first_low, active, bend, part_two, send_two = run_kernel(
        functools.partial(ffn_kernel, sizes),
        [
            shape_of((tokens, width), F32),
            shape_of((tokens, LANES), F32),
            shape_of((tokens, width), BF16),
            shape_of((tokens, ff_half), BF16),
            shape_of((tokens, ff_half), F32),
            shape_of((tokens, width), F32),
            shape_of((tokens, width), BF16),
        ],
        [pooled, mixed, mixed_other, wo_own, wo_other, table, bup, up, down],
        flops=4e9,
    )
    part_other = swap_cores(send_two)
    output, gh2, gsec, ginner, gfirst, gsend, sums_two, gbup = run_kernel(
        functools.partial(ffn_back_kernel, sizes),
        [
            shape_of((row_count * half_length, width), BF16),
            shape_of((tokens, width), F32),
            shape_of((tokens, width), BF16),
            shape_of((tokens, ff_half), BF16),
            shape_of((tokens, width), F32),
            shape_of((tokens, width), BF16),
            shape_of((8, width), F32),
            shape_of((8, ff_half), F32),
        ],
        [act_own, act_other, normed_one, part_two, part_other, table, bend, up, down],
        flops=5e9,
    )
    gfirst_other = swap_cores(gsend)
    gup, gdown = run_kernel(
        ffn_weight_kernel,
        [shape_of((2, width, width), F32), shape_of((ff_half, width), F32)],
        [first_low, active, gsec, ginner],
        flops=3e9,
    )
    by_chips = (dp_size, fsdp_size) == (2, 16)
    if by_chips:
        sum_f = scatter_ffn(gup, gdown, per_row)
    else:
        grad_up, grad_down = scatter_ffn_flat(core, gup, gdown)

    gh1, gq, gk, gv, gwo, sums_one, head_sums = run_kernel(
        functools.partial(attend_back_kernel, sizes),
        [
            shape_of((tokens, width), F32),
            shape_of((rows2, half_length, half), BF16),
            shape_of((rows2, seq_length, half), BF16),
            shape_of((rows2, seq_length, half), BF16),
            shape_of((half, width), F32),
            shape_of((8, width), F32),
            shape_of((8, half), F32),
        ],
        [
            core_at, slopes, act_own, act_other, normed_one, inverse_one, gh2, gfirst, gfirst_other, table, mixed,
            wo_own, q_rows, k_rows, v_rows,
        ],
        [
            pltpu.VMEM((seq_length, half_length), F32),
            pltpu.VMEM((tokens, width), BF16),
            pltpu.VMEM((tokens, half), BF16),
        ],
        scalars=2,
        flops=10e9,
    )
    (grads_a,) = run_kernel(
        functools.partial(attend_weight_kernel, sizes),
        [shape_of((width, 4 * half + LANES), F32)],
        [core_at, act_own, act_other, pooled, gq, gk, gv, gwo, sums_one, sums_two, head_sums, gbup],
        scalars=1,
        flops=4e9,
    )
    if by_chips:
        wide = grads_a.shape[1]
        grads_a = grads_a.reshape((2, 4, 2, 2, per_row, wide))
        sum_a = Chips().scatter(grads_a[0], grads_a[1])
    (inputs_send,) = run_kernel(
        functools.partial(other_inputs_kernel, sizes),
        [shape_of((row_count * seq_length, width), BF16)],
        [gq, gk, gv, wa],
        flops=2e9,
    )
    inputs_other = swap_cores(inputs_send)
    (grad_inputs,) = run_kernel(
        functools.partial(own_inputs_kernel, sizes),
        [shape_of((row_count * seq_length, width), F32)],
        [gq, gk, gv, wa, gh1, inputs_other],
        flops=2e9,
    )

    if by_chips:
        grad_up, grad_down = join_ffn(core, swap_cores, sum_f, per_row)
        grad_q, grad_k, grad_v, grad_o, small = join_attention(core, swap_cores, sum_a)
    else:
        grad_q, grad_k, grad_v, grad_o, small = scatter_attention_flat(core, grads_a)
    small = small.T
    g_bq, g_bv, g_bo, g_g1, g_s1, g_bd, g_g2, g_s2 = (small[i] for i in range(8))
    g_bu = small[8 : 8 + ratio].reshape(per_up)
    return (
        output.reshape(row_count, half_length, width),
        grad_inputs.reshape(row_count, seq_length, width),
        grad_q, g_bq, grad_k, grad_v, g_bv, grad_o, g_bo, g_g1, g_s1, grad_up, g_bu, grad_down, g_bd, g_g2, g_s2,
    )


def solution(mesh):
    rows, matrix, vector = P(AXES, None, None), P(AXES, None), P(AXES)
    in_specs = (
        rows, matrix, matrix, vector, matrix, matrix, vector, matrix, vector, vector, vector, matrix, vector,
        matrix, vector, vector, vector, rows,
    )
    out_specs = (
        rows, rows, matrix, vector, matrix, matrix, vector, matrix, vector, vector, vector, matrix, vector,
        matrix, vector, vector, vector,
    )
    shape = (mesh.shape["dp"], mesh.shape["fsdp"])
    return jax.shard_map(
        functools.partial(body, shape), mesh=mesh, in_specs=in_specs, out_specs=out_specs, check_vma=False
    )
```

```python
import functools
import math

import jax
import jax.numpy as jnp
from jax import lax
from jax.experimental import pallas as pl
from jax.experimental.pallas import tpu as pltpu
from jax.sharding import PartitionSpec as P

HEAD_DIM = 64
LANES = 128
EPSILON = 1e-06
FAR = 1e12
AXES = ("dp", "fsdp")
BF16 = jnp.bfloat16
F32 = jnp.float32
MIB = 1024 * 1024


def nn_dot(left, right):
    return jnp.dot(left, right, preferred_element_type=F32)


def nt_dot(left, right):
    return lax.dot_general(left, right, (((1,), (1,)), ((), ())), preferred_element_type=F32)


def tn_dot(left, right):
    return lax.dot_general(left, right, (((0,), (0,)), ((), ())), preferred_element_type=F32)


def iota(shape, axis):
    return lax.broadcasted_iota(jnp.int32, shape, axis)


def ones_where(condition):
    return jnp.where(condition, 1.0, 0.0).astype(BF16)


def two_parts(array):
    high = array.astype(BF16)
    return high, (array - high.astype(F32)).astype(BF16)


def mean_of(array):
    return jnp.mean(array, axis=-1, keepdims=True)


def gelu_parts(value):
    scale = 0.7978845608028654
    square = value * value
    bend = jnp.tanh(scale * value * (1.0 + 0.044715 * square))
    half = 0.5 * (1.0 + bend)
    slope = half + 0.5 * value * (1.0 - bend * bend) * scale * (1.0 + 3.0 * 0.044715 * square)
    return value * half, slope


COL_BQ, COL_BV, COL_BO, COL_G1, COL_S1, COL_BD, COL_G2, COL_S2, COL_BU = 0, 1, 2, 3, 4, 5, 6, 7, 8


def up_spread(half, ff_half, per_up):
    rows = iota((half, ff_half), 0)
    cols = iota((half, ff_half), 1)
    per_row = half * per_up // ff_half
    same_chip = rows // per_row == cols // per_up
    same_place = rows % per_row == cols % per_row
    return ones_where(same_chip & same_place)


def pack_kernel(core_ref, w_q, w_k, w_v, w_up, b_up, *refs):
    vectors, send_out, own_out, up_out = refs[:8], refs[8], refs[9], refs[10]
    core = core_ref[0]
    per_row, width = w_q.shape
    half = width // 2
    ff_half = w_up.shape[1] // 2
    count = b_up.shape[1]
    table = jnp.concatenate([v[...].astype(F32) for v in vectors] + [jnp.zeros((LANES - 8, per_row), F32)], axis=0)
    eye = ones_where(iota((per_row, per_row), 0) == iota((per_row, per_row), 1))
    shape = (LANES, count)
    spread = jnp.where(iota(shape, 1) // per_row + COL_BU == iota(shape, 0), b_up[...].astype(F32), 0.0)
    fold = ones_where(iota((per_row, count), 1) % per_row == iota((per_row, count), 0))
    biases = (nt_dot(eye, table.astype(BF16)) + nt_dot(fold, spread.astype(BF16))).astype(BF16)
    for out, which in ((send_out, 1 - core), (own_out, core)):
        start = pl.multiple_of(which * half, LANES)
        out[:, :half] = w_q[:, pl.ds(start, half)]
        out[:, half : 2 * half] = w_k[:, pl.ds(start, half)]
        out[:, width : width + LANES] = biases
        out[:, width + LANES : width + LANES + half] = w_v[:, pl.ds(start, half)]
    up_start = pl.multiple_of(core * ff_half, LANES)
    other_start = pl.multiple_of((1 - core) * ff_half, LANES)
    up_out[...] = w_up[:, pl.ds(up_start, ff_half)]
    send_out[:, width + LANES + half :] = w_up[:, pl.ds(other_start, ff_half)]


def chip_pack_kernel(core_ref, own, received, own_up, w_o, w_down, pack_a, pack_f):
    core = core_ref[0]
    width = w_o.shape[1]
    half = width // 2
    base = width + LANES + half
    pack_a[0, :, :base] = own[...]
    pack_a[1, :, :base] = received[:, :base]
    for place, which in ((0, core), (1, 1 - core)):
        start = pl.multiple_of(which * half, LANES)
        pack_a[place, :, base:] = w_o[:, pl.ds(start, half)]
    for part in range(2):
        pack_f[part, 0] = own_up[:, part * width : (part + 1) * width]
        pack_f[part, 1] = received[:, base + part * width : base + (part + 1) * width]
        for place in range(2):
            pack_f[part, 2 + place] = w_down[2 * part + place]


def ready_kernel(sizes, order, act_own, act_other, perm_out, moved_out, pooled_out, pooled_low_out, dm_out, dmt_out, spread_out):
    row_count, seq_length, half_length, width, ff_half, per_up = sizes
    perm_out[...] = ones_where(iota((width, width), 0) == order[0:1, :])
    spread_out[...] = up_spread(width // 2, ff_half, per_up)
    shape, turned = (half_length, seq_length), (seq_length, half_length)
    pool = jnp.where(iota(shape, 1) // 2 == iota(shape, 0), 0.5, 0.0).astype(BF16)
    evens = ones_where(iota(shape, 1) == 2 * iota(shape, 0))
    eye = ones_where(iota((seq_length, seq_length), 0) == iota((seq_length, seq_length), 1))
    distance = jnp.abs((iota(shape, 1) - 2 * iota(shape, 0)).astype(F32) - 0.5)
    distance_t = jnp.abs((iota(turned, 0) - 2 * iota(turned, 1)).astype(F32) - 0.5)
    base = row_count * (seq_length + half_length)
    for row in range(2 * row_count):
        act = act_own if row < row_count else act_other
        local = row % row_count
        hidden = act[local * seq_length : (local + 1) * seq_length, :]
        rows = slice(row * half_length, (row + 1) * half_length)
        pooled = nn_dot(pool, hidden)
        pooled_out[rows, :] = pooled
        pooled_low_out[rows, :] = nn_dot(pooled.astype(BF16), perm_out[...]).astype(BF16)
        moved_out[row] = nn_dot(hidden, perm_out[...]).astype(BF16)
        seg_rows = act[base : base + 16, :seq_length]
        here = slice(local, local + 1)
        seg_query = nt_dot(evens, seg_rows)[:, here]
        dm_out[row] = jnp.where(seg_query == seg_rows[here].astype(F32), distance, FAR)
        seg_key = nt_dot(eye, seg_rows)[:, here]
        dmt_out[row] = jnp.where(seg_key == nt_dot(seg_rows, evens)[here, :], distance_t, FAR)


def pieces_of(one_near, one_far, two_near, two_far, m):
    up, across = divmod(m, 2)
    return (one_near, one_far)[up].at[across], (two_near, two_far)[across].at[up]


def project_kernel(
    sizes, core_ref, moved, pooled_low, perm, spread, one_near, one_far, two_near, two_far,
    q_out, k_out, v_out, wa_out, wo_out, table_out, bup_out, wo_perm, bias_perm,
):
    row_count, seq_length, half_length, width, ff_half, per_up = sizes
    half = width // 2
    block = width // 4
    core = core_ref[0]
    for m in range(4):
        one, two = pieces_of(one_near, one_far, two_near, two_far, m)
        rows = slice(m * block, (m + 1) * block)
        wa_out[rows, :width] = one[:, :width]
        bias_perm[rows, :] = one[:, width:]
        wa_out[rows, width:] = two[:, :half]
        wo_perm[rows, :] = two[:, half:]
    eye = ones_where(iota((16, LANES), 0) == iota((16, LANES), 1))
    table = nt_dot(nt_dot(eye, bias_perm[...]).astype(BF16), perm[...])
    table_out[...] = table
    mine = jnp.where(core == 0, table[:, :half], table[:, half:])
    ups = nn_dot(mine.astype(BF16), spread[...])
    per_row = half * per_up // ff_half
    which = (iota((16, ff_half), 1) % per_up) // per_row + COL_BU
    bup = jnp.sum(jnp.where(iota((16, ff_half), 0) == which, ups, 0.0), axis=0, keepdims=True)
    bup_out[...] = jnp.broadcast_to(bup, (8, ff_half))
    bias_q, bias_v = mine[COL_BQ : COL_BQ + 1], mine[COL_BV : COL_BV + 1]
    for row in range(2 * row_count):
        rows = slice(row * half_length, (row + 1) * half_length)
        query = nn_dot(pooled_low[rows, :], wa_out[:, :half]) + bias_q
        q_out[row] = (query.astype(BF16).astype(F32) * 0.125).astype(BF16)
        k_out[row] = nn_dot(moved[row], wa_out[:, half:width]).astype(BF16)
        v_out[row] = (nn_dot(moved[row], wa_out[:, width:]) + bias_v).astype(BF16)
    for side in range(2):
        wo_out[side] = nn_dot(perm[side * half : (side + 1) * half, :], wo_perm[...]).astype(BF16)


def attend_kernel(sizes, slope_ref, dm, query, key, value, mixed_out):
    row_count, seq_length, half_length, width, ff_half, per_up = sizes
    lane = iota((1, LANES), 1)
    masks = [ones_where(lane < HEAD_DIM), ones_where(lane >= HEAD_DIM)]
    for row in range(2 * row_count):
        for place in range(width // 2 // LANES):
            cols = slice(place * LANES, (place + 1) * LANES)
            q_pair, k_pair, v_pair = query[row, :, cols], key[row, :, cols], value[row, :, cols]
            results = []
            for sub in range(2):
                slope = slope_ref[2 * place + sub]
                scores = nt_dot(q_pair * masks[sub], k_pair) - slope * dm[row]
                peak = jnp.max(scores, axis=-1, keepdims=True)
                raised = jnp.exp(scores - peak)
                total = jnp.sum(raised, axis=-1, keepdims=True)
                probs = (raised * (1.0 / total)).astype(BF16)
                results.append(nn_dot(probs, v_pair))
            mixed_out[row, :, cols] = jnp.where(lane < HEAD_DIM, results[0], results[1]).astype(BF16)


def ffn_up_kernel(
    sizes, pooled, mixed_own, mixed_other, wo_own, wo_other, table, bup, perm,
    one_near, one_far, two_near, two_far,
    normed_out, inverse_out, low_out, active_out, bend_out, up_out,
):
    row_count, seq_length, half_length, width, ff_half, per_up = sizes
    block = width // 4
    for m in range(4):
        for part, piece in enumerate(pieces_of(one_near, one_far, two_near, two_far, m)):
            up_out[part, m * block : (m + 1) * block, :] = piece[...]
    for row in range(2 * row_count):
        rows = slice(row * half_length, (row + 1) * half_length)
        own = mixed_own[row]
        other = mixed_other[(row + row_count) % (2 * row_count)]
        parts = [nn_dot(own, wo_own[side]) + nn_dot(other, wo_other[side]) for side in range(2)]
        hidden = pooled[rows, :] + (jnp.concatenate(parts, axis=1) + table[COL_BO : COL_BO + 1, :])
        center = hidden - mean_of(hidden)
        inverse = lax.rsqrt(mean_of(center * center) + EPSILON)
        normed = center * inverse
        normed_out[rows, :] = normed
        inverse_out[rows, :] = jnp.broadcast_to(inverse, (half_length, LANES))
        first = normed * table[COL_G1 : COL_G1 + 1, :] + table[COL_S1 : COL_S1 + 1, :]
        low_out[rows, :] = nn_dot(first.astype(BF16), perm[...]).astype(BF16)
    chunk = 256
    for start in range(0, ff_half, chunk):
        cols = slice(start, start + chunk)
        side, inside = divmod(start, width)
        inner = nn_dot(low_out[...], up_out[side, :, inside : inside + chunk]) + bup[0:1, cols]
        active, slope = gelu_parts(inner)
        active_out[:, cols] = active.astype(BF16)
        bend_out[:, cols] = slope


def ffn_down_kernel(sizes, chip_ref, active, one_near, one_far, two_near, two_far, send_out, down_out):
    width = sizes[3]
    per_z = width // 16
    for m in range(4):
        for part, piece in enumerate(pieces_of(one_near, one_far, two_near, two_far, m)):
            for z in range(4):
                place = chip_ref[4 * m + z] * (2 * per_z) + part * per_z
                down_out[pl.ds(pl.multiple_of(place, 16), per_z), :] = piece[z * per_z : (z + 1) * per_z, :]
    chunk = 256
    for start in range(0, width, chunk):
        cols = slice(start, start + chunk)
        send_out[:, cols] = nn_dot(active[...], down_out[:, cols]).astype(BF16)


def store_blocks(array, rows_of, part, send_out, keep_out, block):
    for m in range(4):
        up, across = divmod(m, 2)
        leaves, index = (across, up) if part == 0 else (up, across)
        for at, size, rows in rows_of(m):
            value = array[rows, :]
            if leaves:
                send_out[index, at : at + size, :] = value.astype(BF16)
            else:
                keep_out[index, at : at + size, :] = value


def second_norm_kernel(
    sizes, chip_ref, act_own, act_other, normed_one, part_own, part_other, table, active,
    out_out, gh2_out, gsec_out, sums_out, send_one, keep_one, send_two, keep_two, gdown,
):
    row_count, seq_length, half_length, width, ff_half, per_up = sizes
    gain_two = table[COL_G2 : COL_G2 + 1, :]
    zero = jnp.zeros((1, width), F32)
    sum_gain, sum_shift, sum_down = zero, zero, zero
    for row in range(2 * row_count):
        rows = slice(row * half_length, (row + 1) * half_length)
        swapped = (row + row_count) % (2 * row_count)
        other_rows = slice(swapped * half_length, (swapped + 1) * half_length)
        act = act_own if row < row_count else act_other
        base = row_count * seq_length + (row % row_count) * half_length
        first = normed_one[rows, :] * table[COL_G1 : COL_G1 + 1, :] + table[COL_S1 : COL_S1 + 1, :]
        second = part_own[rows, :].astype(F32) + part_other[other_rows, :].astype(F32)
        hidden = first + (second + table[COL_BD : COL_BD + 1, :])
        center = hidden - mean_of(hidden)
        inverse = lax.rsqrt(mean_of(center * center) + EPSILON)
        normed = center * inverse
        if row < row_count:
            out_out[rows, :] = (normed * gain_two + table[COL_S2 : COL_S2 + 1, :]).astype(BF16)
        upstream = act[base : base + half_length, :].astype(F32)
        sum_gain += jnp.sum(upstream * normed, axis=0, keepdims=True)
        sum_shift += jnp.sum(upstream, axis=0, keepdims=True)
        scaled = upstream * gain_two
        grad = inverse * (scaled - mean_of(scaled) - normed * mean_of(scaled * normed))
        gh2_out[rows, :] = grad
        low = grad.astype(BF16)
        gsec_out[rows, :] = low
        sum_down += jnp.sum(low.astype(F32), axis=0, keepdims=True)
    sums_out[...] = jnp.concatenate([sum_gain, sum_shift, sum_down, jnp.zeros((5, width), F32)], axis=0)
    chunk = 256
    for start in range(0, ff_half, chunk):
        gdown[start : start + chunk, :] = tn_dot(active[:, start : start + chunk], gsec_out[...])
    per_z = width // 16
    for part, send_out, keep_out in ((0, send_one, keep_one), (1, send_two, keep_two)):

        def rows_of(m, part=part):
            for z in range(4):
                place = chip_ref[4 * m + z] * (2 * per_z) + part * per_z
                yield z * per_z, per_z, pl.ds(pl.multiple_of(place, 16), per_z)

        store_blocks(gdown, rows_of, part, send_out, keep_out, width // 4)


def ffn_back_kernel(sizes, gsec, bend, perm, up, down, ginner_out, gfirst_out, gbup_out):
    row_count, seq_length, half_length, width, ff_half, per_up = sizes
    chunk = 256
    for start in range(0, ff_half, chunk):
        cols = slice(start, start + chunk)
        grad = (nt_dot(gsec[...], down[cols, :]) * bend[:, cols]).astype(BF16)
        ginner_out[:, cols] = grad
        total = jnp.sum(grad.astype(F32), axis=0, keepdims=True)
        gbup_out[:, cols] = jnp.broadcast_to(total, (8, chunk))
    part = nt_dot(ginner_out[:, :width], up[0]) + nt_dot(ginner_out[:, width:], up[1])
    gfirst_out[...] = nt_dot(part.astype(BF16), perm[...]).astype(BF16)


def ffn_weight_kernel(low, ginner, send_one, keep_one, send_two, keep_two, gup):
    width = low.shape[1]
    block = width // 4
    chunk = 256
    for part, send_out, keep_out in ((0, send_one, keep_one), (1, send_two, keep_two)):
        for start in range(0, width, chunk):
            gup[start : start + chunk, :] = tn_dot(
                low[:, start : start + chunk], ginner[:, part * width : (part + 1) * width]
            )

        def rows_of(m):
            yield 0, block, slice(m * block, (m + 1) * block)

        store_blocks(gup, rows_of, part, send_out, keep_out, block)


def first_norm_kernel(
    sizes, normed_one, inverse_one, gh2, gfirst_own, gfirst_other, table, wo_own,
    gh1_out, gbranch_out, gmixed_out, sums_out,
):
    row_count, seq_length, half_length, width, ff_half, per_up = sizes
    half = width // 2
    gain_one = table[COL_G1 : COL_G1 + 1, :]
    zero = jnp.zeros((1, width), F32)
    sum_gain, sum_shift, sum_out = zero, zero, zero
    for row in range(2 * row_count):
        rows = slice(row * half_length, (row + 1) * half_length)
        swapped = (row + row_count) % (2 * row_count)
        other_rows = slice(swapped * half_length, (swapped + 1) * half_length)
        grad = gh2[rows, :] + (gfirst_own[rows, :].astype(F32) + gfirst_other[other_rows, :].astype(F32))
        normed = normed_one[rows, :]
        sum_gain += jnp.sum(grad * normed, axis=0, keepdims=True)
        sum_shift += jnp.sum(grad, axis=0, keepdims=True)
        scaled = grad * gain_one
        inverse = inverse_one[rows, 0:1]
        grad = inverse * (scaled - mean_of(scaled) - normed * mean_of(scaled * normed))
        if row < row_count:
            gh1_out[rows, :] = grad
        low = grad.astype(BF16)
        gbranch_out[rows, :] = low
        sum_out += jnp.sum(low.astype(F32), axis=0, keepdims=True)
        gmixed_out[row] = (nt_dot(low[:, :half], wo_own[0]) + nt_dot(low[:, half:], wo_own[1])).astype(BF16)
    sums_out[...] = jnp.concatenate([sum_gain, sum_shift, sum_out, jnp.zeros((5, width), F32)], axis=0)


def attend_back_kernel(
    sizes, slope_ref, dmt, gmixed, query, key, value, gq_out, gk_out, gv_out, heads_out,
):
    row_count, seq_length, half_length, width, ff_half, per_up = sizes
    half = width // 2
    lane = iota((1, LANES), 1)
    masks = [ones_where(lane < HEAD_DIM), ones_where(lane >= HEAD_DIM)]
    sums_q = jnp.zeros((1, half), F32)
    sums_v = jnp.zeros((1, half), F32)
    for row in range(2 * row_count):
        for place in range(half // LANES):
            cols = slice(place * LANES, (place + 1) * LANES)
            q_pair, k_pair, v_pair = query[row, :, cols], key[row, :, cols], value[row, :, cols]
            g_pair = gmixed[row, :, cols]
            found = []
            for sub in range(2):
                slope = slope_ref[2 * place + sub]
                scores = nt_dot(k_pair, q_pair * masks[sub]) - slope * dmt[row]
                peak = jnp.max(scores, axis=0, keepdims=True)
                raised = jnp.exp(scores - peak)
                exact = raised * (1.0 / jnp.sum(raised, axis=0, keepdims=True))
                gprobs = nt_dot(v_pair, g_pair * masks[sub])
                mean = jnp.sum(exact * gprobs, axis=0, keepdims=True)
                gscores = (exact * (gprobs - mean)).astype(BF16)
                found.append(
                    (
                        nn_dot(exact.astype(BF16), g_pair),
                        nn_dot(gscores, q_pair),
                        tn_dot(gscores, k_pair) * 0.125,
                    )
                )
            gvalue, gkey, gquery = (
                jnp.where(lane < HEAD_DIM, a, b).astype(BF16) for a, b in zip(found[0], found[1])
            )
            gv_out[row, :, cols] = gvalue
            gk_out[row, :, cols] = gkey
            gq_out[row * half_length : (row + 1) * half_length, cols] = gquery
        sums_q += jnp.sum(gq_out[row * half_length : (row + 1) * half_length, :].astype(F32), axis=0, keepdims=True)
        sums_v += jnp.sum(gv_out[row].astype(F32), axis=0, keepdims=True)
    heads_out[...] = jnp.concatenate([sums_q, sums_v, jnp.zeros((6, half), F32)], axis=0)


def attend_weight_kernel(
    sizes, core_ref, moved, pooled_low, spread, gq, gk, gv, mixed, gbranch, sums_one, sums_two, heads, gbup,
    heads_out, rest_out, send_out,
):
    row_count, seq_length, half_length, width, ff_half, per_up = sizes
    half = width // 2
    core = core_ref[0]
    heads_out[:, :half] = tn_dot(pooled_low[...], gq[...])
    for index, grad in ((1, gk), (2, gv)):
        total = None
        for row in range(2 * row_count):
            term = tn_dot(moved[row], grad[row])
            total = term if total is None else total + term
        heads_out[:, index * half : (index + 1) * half] = total
    per_chip = width // 16
    for chip in range(16):
        rows = slice(chip * per_chip + per_chip // 2, (chip + 1) * per_chip)
        send_out[chip] = heads_out[rows, :].astype(BF16)
    total = None
    for row in range(2 * row_count):
        term = tn_dot(mixed[row], gbranch[row * half_length : (row + 1) * half_length, :])
        total = term if total is None else total + term
    rest_out[:, :width] = total
    mine = [jnp.where(core == 0, sums[:, :half], sums[:, half:]) for sums in (sums_one, sums_two)]
    per_row = half * per_up // ff_half
    which = (iota((8, ff_half), 1) % per_up) // per_row
    high, low = two_parts(jnp.where(iota((8, ff_half), 0) == which, gbup[...], 0.0))
    ups = nt_dot(high, spread[...]) + nt_dot(low, spread[...])
    stacked = jnp.concatenate(
        [
            heads[0:2], mine[0][2:3], mine[0][0:2], mine[1][2:3], mine[1][0:2], ups,
            jnp.zeros((LANES - 16, half), F32),
        ],
        axis=0,
    )
    rest_out[:, width:] = stacked.T


def merge_kernel(core_ref, chip_ref, heads, rest, received, send_one, keep_one, send_two, keep_two):
    core = core_ref[0]
    width = heads.shape[0]
    half = width // 2
    per_row = width // 32
    own = pl.multiple_of(core * half, LANES)
    theirs = pl.multiple_of((1 - core) * half, LANES)
    for m in range(4):
        up, across = divmod(m, 2)
        one, one_at = (send_one, up) if across else (keep_one, up)
        two, two_at = (send_two, across) if up else (keep_two, across)
        for z in range(4):
            chip = 4 * m + z
            mine = heads[chip * 2 * per_row : chip * 2 * per_row + per_row, :]
            got = received[chip].astype(F32)
            place = pl.multiple_of(chip_ref[chip] * per_row, 8)
            outer = rest[pl.ds(place, per_row), :]
            for out, at, index, base in ((one, one_at, 0, 0), (one, one_at, 1, width), (two, two_at, 2, 0)):
                columns = slice(index * half, (index + 1) * half)
                out[at, z, :, pl.ds(base + own, half)] = mine[:, columns].astype(out.dtype)
                out[at, z, :, pl.ds(base + theirs, half)] = got[:, columns].astype(out.dtype)
            one[one_at, z, :, 2 * width :] = outer[:, width:].astype(one.dtype)
            two[two_at, z, :, width:] = outer[:, :width].astype(two.dtype)


def finish_kernel(mine_one, mine_two, first, second, third, q_out, k_out, v_out, o_out, *vectors):
    width = q_out.shape[1]
    per_row = q_out.shape[0]
    split = mine_one.shape[1]

    def total(own, start, size, base):
        terms = [a[:, base + start : base + start + size].astype(F32) for a in (first, second, third)]
        return own[:, start : start + size] + (terms[0] + (terms[1] + terms[2]))

    q_out[...] = total(mine_one, 0, width, 0)
    k_out[...] = total(mine_one, width, width, 0)
    v_out[...] = total(mine_two, 0, width, split)
    o_out[...] = total(mine_two, width, width, split)
    high, low = two_parts(total(mine_one, 2 * width, LANES, 0))
    eye = ones_where(iota((16, LANES), 0) == iota((16, LANES), 1))
    table = nt_dot(eye, high) + nt_dot(eye, low)
    for index in range(8):
        vectors[index][...] = table[index : index + 1, :]
    wide = vectors[8].shape[1]
    high, low = two_parts(table)
    fold = ones_where(iota((per_row, wide), 1) % per_row == iota((per_row, wide), 0))
    spread = nn_dot(high, fold) + nn_dot(low, fold)
    shape = (16, wide)
    picked = jnp.where(iota(shape, 0) == COL_BU + iota(shape, 1) // per_row, spread, 0.0)
    vectors[8][...] = jnp.sum(picked, axis=0, keepdims=True)


def input_grad(sizes, row, gq, gk, gv, wa, perm, extra):
    row_count, seq_length, half_length, width, ff_half, per_up = sizes
    half = width // 2
    grad = nt_dot(gk[row], wa[:, half:width]) + nt_dot(gv[row], wa[:, width:])
    high, low = two_parts(nt_dot(gq[row * half_length : (row + 1) * half_length, :], wa[:, :half]))
    shape = (seq_length, half_length)
    split = jnp.where(iota(shape, 0) // 2 == iota(shape, 1), 0.5, 0.0).astype(BF16)
    grad = grad + (nn_dot(split, high) + nn_dot(split, low))
    if extra is None:
        return nt_dot(grad.astype(BF16), perm[...])
    high, low = two_parts(grad)
    grad = nt_dot(high, perm[...]) + nt_dot(low, perm[...])
    high, low = two_parts(extra)
    return grad + (nn_dot(split, high) + nn_dot(split, low))


def other_inputs_kernel(sizes, gq, gk, gv, wa, perm, send_out):
    row_count, seq_length = sizes[0], sizes[1]
    for local in range(row_count):
        grad = input_grad(sizes, row_count + local, gq, gk, gv, wa, perm, None)
        send_out[local * seq_length : (local + 1) * seq_length, :] = grad.astype(BF16)


def own_inputs_kernel(sizes, gq, gk, gv, wa, perm, gh1, received, grad_out):
    row_count, seq_length, half_length = sizes[0], sizes[1], sizes[2]
    for local in range(row_count):
        extra = gh1[local * half_length : (local + 1) * half_length, :]
        grad = input_grad(sizes, local, gq, gk, gv, wa, perm, extra)
        rows = slice(local * seq_length, (local + 1) * seq_length)
        grad_out[rows, :] = grad + received[rows, :].astype(F32)


def run_kernel(kernel, outs, operands, scratch=(), scalars=0, weight=0.01, spare=8):
    specs = [pl.BlockSpec(memory_space=pltpu.SMEM)] * scalars
    specs += [pl.BlockSpec(memory_space=pltpu.VMEM)] * (len(operands) - scalars)
    moved = sum(a.size * a.dtype.itemsize for a in list(operands) + list(outs))
    held = sum(math.prod(a.shape) * 4 for a in scratch)
    return pl.pallas_call(
        kernel,
        out_shape=tuple(outs),
        in_specs=specs,
        out_specs=tuple(pl.BlockSpec(memory_space=pltpu.VMEM) for _ in outs),
        scratch_shapes=list(scratch),
        compiler_params=pltpu.CompilerParams(vmem_limit_bytes=int(moved * 1.05) + held + spare * MIB),
        cost_estimate=pl.CostEstimate(flops=int(weight * 1e9), bytes_accessed=int(weight * 1e6), transcendentals=0),
    )(*operands)


def shape_of(shape, dtype):
    return jax.ShapeDtypeStruct(shape, dtype)


def shift(array, step):
    return lax.ppermute(array, "fsdp", [(i, (i + 4 * step) % 16) for i in range(16)])


def swap(array, bit):
    return lax.ppermute(array, "fsdp", [(i, i ^ bit) for i in range(16)])


def gather_z(pack):
    return [pack] + [shift(pack, step) for step in (1, 2, 3)]


def near_pieces(one, two):
    return jnp.stack([one, swap(one, 1)], axis=0), jnp.stack([two, swap(two, 2)], axis=0)


def far_pieces(one_near, two_near):
    return swap(one_near, 2), swap(two_near, 1)


def all_pieces(near, far):
    return near[0], far[0], near[1], far[1]


def after(arrays, others):
    return lax.optimization_barrier((arrays, others))[0]


def scatter_near(blocks):
    return swap(blocks[0], 1), swap(blocks[2], 2)


def scatter_far(blocks, got):
    keep_one, keep_two = blocks[1], blocks[3]
    got_one, got_two = got
    next_one = (keep_one[1] + got_one[1].astype(F32)).astype(BF16)
    next_two = (keep_two[1] + got_two[1].astype(F32)).astype(BF16)
    last_one, last_two = swap(next_one, 2), swap(next_two, 1)
    one = keep_one[0] + got_one[0].astype(F32) + last_one.astype(F32)
    two = keep_two[0] + got_two[0].astype(F32) + last_two.astype(F32)
    return one, two


def send_z(parts):
    rows = [a.shape[0] // 4 for a in parts]
    axis = 0 if len({a.shape for a in parts}) == 1 else -1
    received = []
    for step in (1, 2, 3):
        blocks = [a[step * n : (step + 1) * n].astype(BF16) for a, n in zip(parts, rows)]
        received.append(shift(jnp.concatenate(blocks, axis=axis), 4 - step))
    return [a[:n] for a, n in zip(parts, rows)], received


def sum_z(mine, received):
    axis = 0 if len({a.shape for a in mine}) == 1 else -1
    ends = [0]
    for block in mine:
        ends.append(ends[-1] + block.shape[axis])
    return [
        block + sum(lax.slice_in_dim(got, start, end, axis=axis).astype(F32) for got in received)
        for block, start, end in zip(mine, ends, ends[1:])
    ]


def half_columns(array, which):
    size = array.shape[1] // 2
    return lax.dynamic_slice_in_dim(array, which * size, size, axis=1)


def halves(array):
    size = array.shape[1] // 2
    return [array[:, :size], array[:, size:]]


def as_pieces(one, two):
    one, two = (a.reshape((4, a.shape[0] // 4) + a.shape[1:]) for a in (one, two))
    return one[:2], one[2:], two[0::2], two[1::2]


def gather_flat(core, weights):
    w_q, w_k, w_v, w_o, biases, w_up, w_down = (lax.all_gather(w, AXES, axis=0, tiled=True) for w in weights)
    width = w_q.shape[0]
    half = width // 2
    wo = jnp.concatenate(halves(lax.dynamic_slice_in_dim(w_o, core * half, half)), axis=0)
    q, k, v = (half_columns(w, core) for w in (w_q, w_k, w_v))
    pieces_a = as_pieces(jnp.concatenate([q, k, biases], axis=1), jnp.concatenate([v, wo], axis=1))
    up = halves(half_columns(w_up, core))
    ff_half = w_down.shape[0] // 2
    down = lax.dynamic_slice_in_dim(w_down, core * ff_half, ff_half).reshape(16, 2, -1, width)
    return pieces_a, as_pieces(*up), as_pieces(*(down[:, part].reshape(-1, width) for part in range(2)))


def scatter_rows(array):
    return lax.psum_scatter(array, AXES, scatter_dimension=0, tiled=True)


def placed(array, core, axis):
    shape = list(array.shape)
    shape[axis] *= 2
    return lax.dynamic_update_slice_in_dim(jnp.zeros(shape, array.dtype), array, core * array.shape[axis], axis)


def whole_of(blocks):
    send_one, keep_one, send_two, keep_two = (a.astype(F32) for a in blocks)
    one = jnp.stack([keep_one, send_one], axis=1)
    two = jnp.stack([keep_two, send_two], axis=0)
    return [a.reshape((-1,) + a.shape[3:]) for a in (one, two)]


def scatter_ffn_flat(core, up_blocks, down_blocks):
    up = placed(jnp.concatenate(whole_of(up_blocks), axis=1), core, 1)
    one, two = whole_of(down_blocks)
    width = one.shape[1]
    down = jnp.stack([one.reshape(16, -1, width), two.reshape(16, -1, width)], axis=1).reshape(-1, width)
    return scatter_rows(up), scatter_rows(placed(down, core, 0))


def scatter_attention_flat(core, heads, rest):
    width = heads.shape[0]
    half = width // 2
    found = [scatter_rows(placed(heads[:, i * half : (i + 1) * half], core, 1)) for i in range(3)]
    return found + [scatter_rows(placed(a, core, 0)) for a in (rest[:, :width], rest[:, width:])]


def body(mesh_shape, *args):
    (
        inputs, segments, w_q, b_q, w_k, w_v, b_v, w_o, b_o, ln1_gain, ln1_bias, w_up, b_up, w_down,
        b_down, ln2_gain, ln2_bias, grad_out,
    ) = args
    dp_size, fsdp_size = mesh_shape
    by_chips = (dp_size, fsdp_size) == (2, 16)
    row_count, seq_length, width = inputs.shape
    half_length = seq_length // 2
    half = width // 2
    per_row, ff = w_up.shape
    ff_half = ff // 2
    per_up = w_down.shape[0]
    ratio = per_up // per_row
    rows2 = 2 * row_count
    tokens = rows2 * half_length
    core = lax.axis_index("dp") & 1
    core_at = core.reshape(1).astype(jnp.int32)
    heads = width // HEAD_DIM
    slopes = 2.0 ** (-8.0 * (jnp.arange(heads, dtype=F32) + 1.0) / heads)
    slopes = jnp.where(core == 0, slopes[: heads // 2], slopes[heads // 2 :])
    swap_pairs = [(i, i ^ 1) for i in range(dp_size)]

    def swap_cores(array):
        return lax.ppermute(array, "dp", swap_pairs)

    place = jnp.arange(width, dtype=jnp.int32)
    if by_chips:
        index = lax.axis_index("fsdp")
        z, yx = index >> 2, index & 3
        m, s = place // (width // 4), place // (width // 16) % 4
        chip = 4 * ((z - s) & 3) + (yx ^ m)
        order = (core ^ (place // per_row % 2)) * half + chip * per_row + place % per_row
        number = jnp.arange(16, dtype=jnp.int32)
        chip_at = 4 * ((z - number) & 3) + (yx ^ (number // 4))
        spread_rows = per_up
    else:
        order, chip_at, spread_rows = place, jnp.arange(16, dtype=jnp.int32), per_up
    sizes = (row_count, seq_length, half_length, width, ff_half, spread_rows)
    order = jnp.broadcast_to(order, (8, width)).astype(jnp.int32)

    vectors = (b_q, b_v, b_o, ln1_gain, ln1_bias, b_down, ln2_gain, ln2_bias)
    seg_rows = jnp.pad(segments.astype(BF16), ((0, 16 - row_count), (0, width - seq_length)))
    act_own = jnp.concatenate(
        [inputs.reshape(-1, width), grad_out.reshape(-1, width), seg_rows], axis=0
    )
    act_other = swap_cores(act_own)

    def prepare(acts):
        return run_kernel(
            functools.partial(ready_kernel, sizes),
            [
                shape_of((width, width), BF16),
                shape_of((rows2, seq_length, width), BF16),
                shape_of((tokens, width), F32),
                shape_of((tokens, width), BF16),
                shape_of((rows2, half_length, seq_length), F32),
                shape_of((rows2, seq_length, half_length), F32),
                shape_of((half, ff_half), BF16),
            ],
            [order, *acts],
            weight=20,
        )

    if by_chips:
        base = width + LANES + half
        send, own, own_up = run_kernel(
            pack_kernel,
            [shape_of((per_row, base + ff_half), BF16), shape_of((per_row, base), BF16), shape_of((per_row, ff_half), BF16)],
            [core_at, w_q, w_k, w_v, w_up, b_up.reshape(1, -1)] + [v.reshape(1, -1) for v in vectors],
            scalars=1,
            spare=54,
        )
        received = swap_cores(send)
        pack_a, pack_f = run_kernel(
            chip_pack_kernel,
            [shape_of((2, per_row, base + half), BF16), shape_of((2, 4, per_row, width), BF16)],
            [core_at, own, received, own_up, w_o, w_down.reshape(4, per_row, width)],
            scalars=1,
            spare=54,
        )
        around = gather_z(after(pack_a, act_other).reshape(2 * per_row, base + half))
        split = width + LANES
        one = jnp.concatenate([a[:, :split] for a in around], axis=0)
        two = jnp.concatenate([a[:, split:] for a in around], axis=0)
        near_a = near_pieces(one, two)
        around = gather_z(after(pack_f, (one, two)).reshape(2, 4 * per_row, width))
        far_a = far_pieces(*near_a)
        perm, *prepared = prepare(after((act_own, act_other), near_a))
        around = after(around, perm)
        ups = [jnp.concatenate([a[part, : 2 * per_row] for a in around], axis=0) for part in range(2)]
        downs = [jnp.concatenate([a[part, 2 * per_row :] for a in around], axis=0) for part in range(2)]
        far_a = after(far_a, (ups, downs))
        pieces_a = all_pieces(near_a, far_a)
        near_up = near_pieces(*ups)
        pieces_up = all_pieces(near_up, far_pieces(*near_up))
        near_down = near_pieces(*after(downs, near_up))
        pieces_down = all_pieces(near_down, far_pieces(*near_down))
    else:
        biases = jnp.stack(vectors, axis=0)
        biases = jnp.concatenate([biases, b_up.reshape(ratio, per_row)], axis=0)
        biases = jnp.pad(biases, ((0, LANES - 8 - ratio), (0, 0))).T
        perm, *prepared = prepare((act_own, act_other))
        near_up, (pieces_a, pieces_up, pieces_down) = (), gather_flat(core, (w_q, w_k, w_v, w_o, biases, w_up, w_down))
    moved, pooled, pooled_low, dm, dmt, spread = prepared
    q_rows, k_rows, v_rows, wa, wo_own, table, bup = run_kernel(
        functools.partial(project_kernel, sizes),
        [
            shape_of((rows2, half_length, half), BF16),
            shape_of((rows2, seq_length, half), BF16),
            shape_of((rows2, seq_length, half), BF16),
            shape_of((width, 3 * half), BF16),
            shape_of((2, half, half), BF16),
            shape_of((16, width), F32),
            shape_of((8, ff_half), F32),
        ],
        [core_at, moved, pooled_low, perm, spread, *pieces_a],
        [pltpu.VMEM((width, half), BF16), pltpu.VMEM((width, LANES), BF16)],
        scalars=1,
    )
    (mixed,) = run_kernel(
        functools.partial(attend_kernel, sizes),
        [shape_of((rows2, half_length, half), BF16)],
        [slopes, dm, after(q_rows, near_up), k_rows, v_rows],
        scalars=1,
    )
    wo_other = swap_cores(wo_own)
    mixed_other = swap_cores(mixed)
    normed_one, inverse_one, first_low, active, bend, up = run_kernel(
        functools.partial(ffn_up_kernel, sizes),
        [
            shape_of((tokens, width), F32),
            shape_of((tokens, LANES), F32),
            shape_of((tokens, width), BF16),
            shape_of((tokens, ff_half), BF16),
            shape_of((tokens, ff_half), F32),
            shape_of((2, width, width), BF16),
        ],
        [pooled, mixed, mixed_other, wo_own, wo_other, table, bup, perm, *pieces_up],
    )
    part_two, down = run_kernel(
        functools.partial(ffn_down_kernel, sizes),
        [shape_of((tokens, width), BF16), shape_of((ff_half, width), BF16)],
        [chip_at, active, *pieces_down],
        scalars=1,
    )
    part_other = swap_cores(part_two)
    block = width // 4
    send_shape, keep_shape = shape_of((2, block, width), BF16), shape_of((2, block, width), F32)
    output, gh2, gsec, sums_two, *down_blocks = run_kernel(
        functools.partial(second_norm_kernel, sizes),
        [
            shape_of((row_count * half_length, width), BF16),
            shape_of((tokens, width), F32),
            shape_of((tokens, width), BF16),
            shape_of((8, width), F32),
            send_shape, keep_shape, send_shape, keep_shape,
        ],
        [chip_at, act_own, act_other, normed_one, part_two, part_other, table, active],
        [pltpu.VMEM((ff_half, width), F32)],
        scalars=1,
    )
    ginner, gfirst, gbup = run_kernel(
        functools.partial(ffn_back_kernel, sizes),
        [shape_of((tokens, ff_half), BF16), shape_of((tokens, width), BF16), shape_of((8, ff_half), F32)],
        [gsec, bend, perm, up, down],
    )
    gfirst_other = swap_cores(gfirst)
    up_blocks = run_kernel(
        ffn_weight_kernel,
        [send_shape, keep_shape, send_shape, keep_shape],
        [first_low, ginner],
        [pltpu.VMEM((width, width), F32)],
    )
    gh1, gbranch, gmixed, sums_one = run_kernel(
        functools.partial(first_norm_kernel, sizes),
        [
            shape_of((row_count * half_length, width), F32),
            shape_of((tokens, width), BF16),
            shape_of((rows2, half_length, half), BF16),
            shape_of((8, width), F32),
        ],
        [normed_one, inverse_one, gh2, gfirst, gfirst_other, table, wo_own],
    )
    gq, gk, gv, head_sums = run_kernel(
        functools.partial(attend_back_kernel, sizes),
        [
            shape_of((tokens, half), BF16),
            shape_of((rows2, seq_length, half), BF16),
            shape_of((rows2, seq_length, half), BF16),
            shape_of((8, half), F32),
        ],
        [slopes, dmt, gmixed, q_rows, k_rows, v_rows],
        scalars=1,
    )
    grad_heads, grad_rest, heads_send = run_kernel(
        functools.partial(attend_weight_kernel, sizes),
        [
            shape_of((width, 3 * half), F32),
            shape_of((half, width + LANES), F32),
            shape_of((16, width // 32, 3 * half), BF16),
        ],
        [core_at, moved, pooled_low, spread, gq, gk, gv, mixed, gbranch, sums_one, sums_two, head_sums, gbup],
        scalars=1,
    )
    if by_chips:
        down_parts = scatter_far(down_blocks, after(scatter_near(down_blocks), gq))
        heads_other = swap_cores(heads_send)
        blocks = (4, per_row)
        columns_one, columns_two = 2 * width + LANES, 2 * width
        attend_blocks = run_kernel(
            merge_kernel,
            [
                shape_of((2,) + blocks + (columns_one,), BF16),
                shape_of((2,) + blocks + (columns_one,), F32),
                shape_of((2,) + blocks + (columns_two,), BF16),
                shape_of((2,) + blocks + (columns_two,), F32),
            ],
            [core_at, chip_at, grad_heads, grad_rest, heads_other],
            scalars=2,
        )
        got_up = after(scatter_near(up_blocks), tuple(attend_blocks))
        attend_blocks = after(tuple(attend_blocks), (got_up, down_parts))
        up_parts = scatter_far(up_blocks, got_up)
        got_attend = scatter_near(attend_blocks)
        gq = after(gq, up_parts)
    (inputs_send,) = run_kernel(
        functools.partial(other_inputs_kernel, sizes),
        [shape_of((row_count * seq_length, width), BF16)],
        [gq, gk, gv, wa, perm],
    )
    if by_chips:
        parts_f, z_blocks = send_z([*down_parts, *up_parts])
        parts_a = scatter_far(attend_blocks, got_attend)
        inputs_send = after(inputs_send, parts_a)
    inputs_other = swap_cores(inputs_send)
    (grad_inputs,) = run_kernel(
        functools.partial(own_inputs_kernel, sizes),
        [shape_of((row_count * seq_length, width), F32)],
        [gq, gk, gv, wa, perm, gh1, inputs_other],
    )
    if by_chips:
        z_blocks = after(z_blocks, parts_a)
        down_one, down_two, up_one, up_two = sum_z(parts_f, z_blocks)
        grad_down = jnp.concatenate([down_one, down_two], axis=0)
        up_got = swap_cores(jnp.concatenate([up_one[per_row:], up_two[per_row:]], axis=1))
        up_mine = jnp.concatenate([up_one[:per_row], up_two[:per_row]], axis=1)
        grad_up = jnp.where(
            core == 0, jnp.concatenate([up_mine, up_got], -1), jnp.concatenate([up_got, up_mine], -1)
        )
        mine, received = send_z(list(parts_a))
        received = after(received, (grad_inputs, grad_up, grad_down))
        square, vector = shape_of((per_row, width), F32), shape_of((1, per_row), F32)
        found = run_kernel(
            finish_kernel,
            [square] * 4 + [vector] * 8 + [shape_of((1, per_up), F32)],
            [a.reshape(per_row, -1) for a in (*mine, *received)],
        )
        grad_q, grad_k, grad_v, grad_o = found[:4]
        g_bq, g_bv, g_bo, g_g1, g_s1, g_bd, g_g2, g_s2, g_bu = (a.reshape(-1) for a in found[4:])
    else:
        grad_up, grad_down = scatter_ffn_flat(core, up_blocks, down_blocks)
        found = scatter_attention_flat(core, grad_heads, grad_rest)
        grad_q, grad_k, grad_v, grad_o = found[:4]
        small = found[4].T
        g_bq, g_bv, g_bo, g_g1, g_s1, g_bd, g_g2, g_s2 = (small[i] for i in range(8))
        g_bu = small[8 : 8 + ratio].reshape(per_up)
    return (
        output.reshape(row_count, half_length, width),
        grad_inputs.reshape(row_count, seq_length, width),
        grad_q, g_bq, grad_k, grad_v, g_bv, grad_o, g_bo, g_g1, g_s1, grad_up, g_bu, grad_down, g_bd, g_g2, g_s2,
    )


def solution(mesh):
    rows, matrix, vector = P(AXES, None, None), P(AXES, None), P(AXES)
    in_specs = (
        rows, matrix, matrix, vector, matrix, matrix, vector, matrix, vector, vector, vector, matrix, vector,
        matrix, vector, vector, vector, rows,
    )
    out_specs = (
        rows, rows, matrix, vector, matrix, matrix, vector, matrix, vector, vector, vector, matrix, vector,
        matrix, vector, vector, vector,
    )
    shape = (mesh.shape["dp"], mesh.shape["fsdp"])
    return jax.shard_map(
        functools.partial(body, shape), mesh=mesh, in_specs=in_specs, out_specs=out_specs, check_vma=False
    )
```

```python
import functools
import math

import jax
import jax.numpy as jnp
from jax import lax
from jax.experimental import pallas as pl
from jax.experimental.pallas import tpu as pltpu
from jax.sharding import PartitionSpec as P

HEAD_DIM = 64
LANES = 128
EPSILON = 1e-06
FAR = 1e12
AXES = ("dp", "fsdp")
BF16 = jnp.bfloat16
F32 = jnp.float32
MIB = 1024 * 1024


def nn_dot(left, right):
    return jnp.dot(left, right, preferred_element_type=F32)


def nt_dot(left, right):
    return lax.dot_general(left, right, (((1,), (1,)), ((), ())), preferred_element_type=F32)


def tn_dot(left, right):
    return lax.dot_general(left, right, (((0,), (0,)), ((), ())), preferred_element_type=F32)


def iota(shape, axis):
    return lax.broadcasted_iota(jnp.int32, shape, axis)


def ones_where(condition):
    return jnp.where(condition, 1.0, 0.0).astype(BF16)


def two_parts(array):
    high = array.astype(BF16)
    return high, (array - high.astype(F32)).astype(BF16)


def mean_of(array):
    return jnp.mean(array, axis=-1, keepdims=True)


def gelu_parts(value):
    scale = 0.7978845608028654
    square = value * value
    bend = jnp.tanh(scale * value * (1.0 + 0.044715 * square))
    half = 0.5 * (1.0 + bend)
    slope = half + 0.5 * value * (1.0 - bend * bend) * scale * (1.0 + 3.0 * 0.044715 * square)
    return value * half, slope


COL_BQ, COL_BV, COL_BO, COL_G1, COL_S1, COL_BD, COL_G2, COL_S2, COL_BU = 0, 1, 2, 3, 4, 5, 6, 7, 8


def up_spread(half, ff_half, per_up):
    rows = iota((half, ff_half), 0)
    cols = iota((half, ff_half), 1)
    per_row = half * per_up // ff_half
    same_chip = rows // per_row == cols // per_up
    same_place = rows % per_row == cols % per_row
    return ones_where(same_chip & same_place)


def pack_kernel(core_ref, w_q, w_k, w_v, w_up, b_up, *refs):
    vectors, send_out, own_out, up_out = refs[:8], refs[8], refs[9], refs[10]
    core = core_ref[0]
    per_row, width = w_q.shape
    half = width // 2
    ff_half = w_up.shape[1] // 2
    count = b_up.shape[1]
    table = jnp.concatenate([v[...].astype(F32) for v in vectors] + [jnp.zeros((LANES - 8, per_row), F32)], axis=0)
    eye = ones_where(iota((per_row, per_row), 0) == iota((per_row, per_row), 1))
    shape = (LANES, count)
    spread = jnp.where(iota(shape, 1) // per_row + COL_BU == iota(shape, 0), b_up[...].astype(F32), 0.0)
    fold = ones_where(iota((per_row, count), 1) % per_row == iota((per_row, count), 0))
    biases = (nt_dot(eye, table.astype(BF16)) + nt_dot(fold, spread.astype(BF16))).astype(BF16)
    for out, which in ((send_out, 1 - core), (own_out, core)):
        start = pl.multiple_of(which * half, LANES)
        out[:, :half] = w_q[:, pl.ds(start, half)]
        out[:, half : 2 * half] = w_k[:, pl.ds(start, half)]
        out[:, width : width + LANES] = biases
        out[:, width + LANES : width + LANES + half] = w_v[:, pl.ds(start, half)]
    up_start = pl.multiple_of(core * ff_half, LANES)
    other_start = pl.multiple_of((1 - core) * ff_half, LANES)
    up_out[...] = w_up[:, pl.ds(up_start, ff_half)]
    send_out[:, width + LANES + half :] = w_up[:, pl.ds(other_start, ff_half)]


def chip_pack_kernel(core_ref, own, received, own_up, w_o, pack_a, pack_up):
    core = core_ref[0]
    width = w_o.shape[1]
    half = width // 2
    base = width + LANES + half
    pack_a[0, :, :base] = own[...]
    pack_a[1, :, :base] = received[:, :base]
    for place, which in ((0, core), (1, 1 - core)):
        start = pl.multiple_of(which * half, LANES)
        pack_a[place, :, base:] = w_o[:, pl.ds(start, half)]
    for part in range(2):
        pack_up[part, 0] = own_up[:, part * width : (part + 1) * width]
        pack_up[part, 1] = received[:, base + part * width : base + (part + 1) * width]


def ready_kernel(sizes, order, act_own, act_other, perm_out, moved_out, pooled_out, pooled_low_out, dm_out, dmt_out, spread_out):
    row_count, seq_length, half_length, width, ff_half, per_up = sizes
    perm_out[...] = ones_where(iota((width, width), 0) == order[0:1, :])
    spread_out[...] = up_spread(width // 2, ff_half, per_up)
    shape, turned = (half_length, seq_length), (seq_length, half_length)
    pool = jnp.where(iota(shape, 1) // 2 == iota(shape, 0), 0.5, 0.0).astype(BF16)
    evens = ones_where(iota(shape, 1) == 2 * iota(shape, 0))
    eye = ones_where(iota((seq_length, seq_length), 0) == iota((seq_length, seq_length), 1))
    distance = jnp.abs((iota(shape, 1) - 2 * iota(shape, 0)).astype(F32) - 0.5)
    distance_t = jnp.abs((iota(turned, 0) - 2 * iota(turned, 1)).astype(F32) - 0.5)
    base = row_count * (seq_length + half_length)
    for row in range(2 * row_count):
        act = act_own if row < row_count else act_other
        local = row % row_count
        hidden = act[local * seq_length : (local + 1) * seq_length, :]
        rows = slice(row * half_length, (row + 1) * half_length)
        pooled = nn_dot(pool, hidden)
        pooled_out[rows, :] = pooled
        pooled_low_out[rows, :] = nn_dot(pooled.astype(BF16), perm_out[...]).astype(BF16)
        moved_out[row] = nn_dot(hidden, perm_out[...]).astype(BF16)
        seg_rows = act[base : base + 16, :seq_length]
        here = slice(local, local + 1)
        seg_query = nt_dot(evens, seg_rows)[:, here]
        dm_out[row] = jnp.where(seg_query == seg_rows[here].astype(F32), distance, FAR)
        seg_key = nt_dot(eye, seg_rows)[:, here]
        dmt_out[row] = jnp.where(seg_key == nt_dot(seg_rows, evens)[here, :], distance_t, FAR)


def pieces_of(one_near, one_far, two_near, two_far, m):
    up, across = divmod(m, 2)
    return (one_near, one_far)[up].at[across], (two_near, two_far)[across].at[up]


def project_kernel(
    sizes, core_ref, moved, pooled_low, perm, spread, one_near, one_far, two_near, two_far,
    q_out, k_out, v_out, wa_out, wo_out, table_out, bup_out, wo_perm, bias_perm,
):
    row_count, seq_length, half_length, width, ff_half, per_up = sizes
    half = width // 2
    block = width // 4
    core = core_ref[0]
    for m in range(4):
        one, two = pieces_of(one_near, one_far, two_near, two_far, m)
        rows = slice(m * block, (m + 1) * block)
        wa_out[rows, :width] = one[:, :width]
        bias_perm[rows, :] = one[:, width:]
        wa_out[rows, width:] = two[:, :half]
        wo_perm[rows, :] = two[:, half:]
    eye = ones_where(iota((16, LANES), 0) == iota((16, LANES), 1))
    table = nt_dot(nt_dot(eye, bias_perm[...]).astype(BF16), perm[...])
    table_out[...] = table
    mine = jnp.where(core == 0, table[:, :half], table[:, half:])
    ups = nn_dot(mine.astype(BF16), spread[...])
    per_row = half * per_up // ff_half
    which = (iota((16, ff_half), 1) % per_up) // per_row + COL_BU
    bup = jnp.sum(jnp.where(iota((16, ff_half), 0) == which, ups, 0.0), axis=0, keepdims=True)
    bup_out[...] = jnp.broadcast_to(bup, (8, ff_half))
    bias_q, bias_v = mine[COL_BQ : COL_BQ + 1], mine[COL_BV : COL_BV + 1]
    for row in range(2 * row_count):
        rows = slice(row * half_length, (row + 1) * half_length)
        query = nn_dot(pooled_low[rows, :], wa_out[:, :half]) + bias_q
        q_out[row] = (query.astype(BF16).astype(F32) * 0.125).astype(BF16)
        k_out[row] = nn_dot(moved[row], wa_out[:, half:width]).astype(BF16)
        v_out[row] = (nn_dot(moved[row], wa_out[:, width:]) + bias_v).astype(BF16)
    for side in range(2):
        wo_out[side] = nn_dot(perm[side * half : (side + 1) * half, :], wo_perm[...]).astype(BF16)


def attend_kernel(sizes, slope_ref, dm, query, key, value, mixed_out):
    row_count, seq_length, half_length, width, ff_half, per_up = sizes
    lane = iota((1, LANES), 1)
    masks = [ones_where(lane < HEAD_DIM), ones_where(lane >= HEAD_DIM)]
    for row in range(2 * row_count):
        for place in range(width // 2 // LANES):
            cols = slice(place * LANES, (place + 1) * LANES)
            q_pair, k_pair, v_pair = query[row, :, cols], key[row, :, cols], value[row, :, cols]
            results = []
            for sub in range(2):
                slope = slope_ref[2 * place + sub]
                scores = nt_dot(q_pair * masks[sub], k_pair) - slope * dm[row]
                peak = jnp.max(scores, axis=-1, keepdims=True)
                raised = jnp.exp(scores - peak)
                total = jnp.sum(raised, axis=-1, keepdims=True)
                probs = (raised * (1.0 / total)).astype(BF16)
                results.append(nn_dot(probs, v_pair))
            mixed_out[row, :, cols] = jnp.where(lane < HEAD_DIM, results[0], results[1]).astype(BF16)


def ffn_up_kernel(
    sizes, pooled, mixed_own, mixed_other, wo_own, wo_other, table, bup, perm,
    one_near, one_far, two_near, two_far,
    normed_out, inverse_out, low_out, active_out, bend_out, up_out,
):
    row_count, seq_length, half_length, width, ff_half, per_up = sizes
    block = width // 4
    for m in range(4):
        for part, piece in enumerate(pieces_of(one_near, one_far, two_near, two_far, m)):
            up_out[part, m * block : (m + 1) * block, :] = piece[...]
    for row in range(2 * row_count):
        rows = slice(row * half_length, (row + 1) * half_length)
        own = mixed_own[row]
        other = mixed_other[(row + row_count) % (2 * row_count)]
        parts = [nn_dot(own, wo_own[side]) + nn_dot(other, wo_other[side]) for side in range(2)]
        hidden = pooled[rows, :] + (jnp.concatenate(parts, axis=1) + table[COL_BO : COL_BO + 1, :])
        center = hidden - mean_of(hidden)
        inverse = lax.rsqrt(mean_of(center * center) + EPSILON)
        normed = center * inverse
        normed_out[rows, :] = normed
        inverse_out[rows, :] = jnp.broadcast_to(inverse, (half_length, LANES))
        first = normed * table[COL_G1 : COL_G1 + 1, :] + table[COL_S1 : COL_S1 + 1, :]
        low_out[rows, :] = nn_dot(first.astype(BF16), perm[...]).astype(BF16)
    chunk = 256
    for start in range(0, ff_half, chunk):
        cols = slice(start, start + chunk)
        side, inside = divmod(start, width)
        inner = nn_dot(low_out[...], up_out[side, :, inside : inside + chunk]) + bup[0:1, cols]
        active, slope = gelu_parts(inner)
        active_out[:, cols] = active.astype(BF16)
        bend_out[:, cols] = slope


def ffn_down_kernel(sizes, chip_ref, active, one_near, one_far, two_near, two_far, send_out, down_out):
    width = sizes[3]
    per_z = width // 16
    for m in range(4):
        for part, piece in enumerate(pieces_of(one_near, one_far, two_near, two_far, m)):
            for z in range(4):
                place = chip_ref[4 * m + z] * (2 * per_z) + part * per_z
                down_out[pl.ds(pl.multiple_of(place, 16), per_z), :] = piece[z * per_z : (z + 1) * per_z, :]
    chunk = 256
    for start in range(0, width, chunk):
        cols = slice(start, start + chunk)
        send_out[:, cols] = nn_dot(active[...], down_out[:, cols]).astype(BF16)


def store_blocks(array, rows_of, part, send_out, keep_out, block):
    for m in range(4):
        up, across = divmod(m, 2)
        leaves, index = (across, up) if part == 0 else (up, across)
        for at, size, rows in rows_of(m):
            value = array[rows, :]
            if leaves:
                send_out[index, at : at + size, :] = value.astype(BF16)
            else:
                keep_out[index, at : at + size, :] = value


def second_norm_kernel(
    sizes, chip_ref, act_own, act_other, normed_one, part_own, part_other, table, active,
    out_out, gh2_out, gsec_out, sums_out, send_one, keep_one, send_two, keep_two, gdown,
):
    row_count, seq_length, half_length, width, ff_half, per_up = sizes
    gain_two = table[COL_G2 : COL_G2 + 1, :]
    zero = jnp.zeros((1, width), F32)
    sum_gain, sum_shift, sum_down = zero, zero, zero
    for row in range(2 * row_count):
        rows = slice(row * half_length, (row + 1) * half_length)
        swapped = (row + row_count) % (2 * row_count)
        other_rows = slice(swapped * half_length, (swapped + 1) * half_length)
        act = act_own if row < row_count else act_other
        base = row_count * seq_length + (row % row_count) * half_length
        first = normed_one[rows, :] * table[COL_G1 : COL_G1 + 1, :] + table[COL_S1 : COL_S1 + 1, :]
        second = part_own[rows, :].astype(F32) + part_other[other_rows, :].astype(F32)
        hidden = first + (second + table[COL_BD : COL_BD + 1, :])
        center = hidden - mean_of(hidden)
        inverse = lax.rsqrt(mean_of(center * center) + EPSILON)
        normed = center * inverse
        if row < row_count:
            out_out[rows, :] = (normed * gain_two + table[COL_S2 : COL_S2 + 1, :]).astype(BF16)
        upstream = act[base : base + half_length, :].astype(F32)
        sum_gain += jnp.sum(upstream * normed, axis=0, keepdims=True)
        sum_shift += jnp.sum(upstream, axis=0, keepdims=True)
        scaled = upstream * gain_two
        grad = inverse * (scaled - mean_of(scaled) - normed * mean_of(scaled * normed))
        gh2_out[rows, :] = grad
        low = grad.astype(BF16)
        gsec_out[rows, :] = low
        sum_down += jnp.sum(low.astype(F32), axis=0, keepdims=True)
    sums_out[...] = jnp.concatenate([sum_gain, sum_shift, sum_down, jnp.zeros((5, width), F32)], axis=0)
    chunk = 256
    for start in range(0, ff_half, chunk):
        gdown[start : start + chunk, :] = tn_dot(active[:, start : start + chunk], gsec_out[...])
    per_z = width // 16
    for part, send_out, keep_out in ((0, send_one, keep_one), (1, send_two, keep_two)):

        def rows_of(m, part=part):
            for z in range(4):
                place = chip_ref[4 * m + z] * (2 * per_z) + part * per_z
                yield z * per_z, per_z, pl.ds(pl.multiple_of(place, 16), per_z)

        store_blocks(gdown, rows_of, part, send_out, keep_out, width // 4)


def ffn_back_kernel(sizes, gsec, bend, perm, up, down, ginner_out, gfirst_out, gbup_out):
    row_count, seq_length, half_length, width, ff_half, per_up = sizes
    chunk = 256
    for start in range(0, ff_half, chunk):
        cols = slice(start, start + chunk)
        grad = (nt_dot(gsec[...], down[cols, :]) * bend[:, cols]).astype(BF16)
        ginner_out[:, cols] = grad
        total = jnp.sum(grad.astype(F32), axis=0, keepdims=True)
        gbup_out[:, cols] = jnp.broadcast_to(total, (8, chunk))
    part = nt_dot(ginner_out[:, :width], up[0]) + nt_dot(ginner_out[:, width:], up[1])
    gfirst_out[...] = nt_dot(part.astype(BF16), perm[...]).astype(BF16)


def ffn_weight_kernel(turn_ref, low, ginner, send_one, keep_one, send_two, keep_two, gup):
    width = low.shape[1]
    block = width // 4
    chunk = 256
    for part, send_out, keep_out in ((0, send_one, keep_one), (1, send_two, keep_two)):
        for start in range(0, width, chunk):
            gup[start : start + chunk, :] = tn_dot(
                low[:, start : start + chunk], ginner[:, part * width : (part + 1) * width]
            )

        def rows_of(m):
            per_z = block // 4
            for z in range(4):
                place = m * block + turn_ref[z] * per_z
                yield z * per_z, per_z, pl.ds(pl.multiple_of(place, 16), per_z)

        store_blocks(gup, rows_of, part, send_out, keep_out, block)


def first_norm_kernel(
    sizes, normed_one, inverse_one, gh2, gfirst_own, gfirst_other, table, wo_own,
    gh1_out, gbranch_out, gmixed_out, sums_out,
):
    row_count, seq_length, half_length, width, ff_half, per_up = sizes
    half = width // 2
    gain_one = table[COL_G1 : COL_G1 + 1, :]
    zero = jnp.zeros((1, width), F32)
    sum_gain, sum_shift, sum_out = zero, zero, zero
    for row in range(2 * row_count):
        rows = slice(row * half_length, (row + 1) * half_length)
        swapped = (row + row_count) % (2 * row_count)
        other_rows = slice(swapped * half_length, (swapped + 1) * half_length)
        grad = gh2[rows, :] + (gfirst_own[rows, :].astype(F32) + gfirst_other[other_rows, :].astype(F32))
        normed = normed_one[rows, :]
        sum_gain += jnp.sum(grad * normed, axis=0, keepdims=True)
        sum_shift += jnp.sum(grad, axis=0, keepdims=True)
        scaled = grad * gain_one
        inverse = inverse_one[rows, 0:1]
        grad = inverse * (scaled - mean_of(scaled) - normed * mean_of(scaled * normed))
        if row < row_count:
            gh1_out[rows, :] = grad
        low = grad.astype(BF16)
        gbranch_out[rows, :] = low
        sum_out += jnp.sum(low.astype(F32), axis=0, keepdims=True)
        gmixed_out[row] = (nt_dot(low[:, :half], wo_own[0]) + nt_dot(low[:, half:], wo_own[1])).astype(BF16)
    sums_out[...] = jnp.concatenate([sum_gain, sum_shift, sum_out, jnp.zeros((5, width), F32)], axis=0)


def attend_back_kernel(
    sizes, slope_ref, dmt, gmixed, query, key, value, gq_out, gk_out, gv_out, heads_out,
):
    row_count, seq_length, half_length, width, ff_half, per_up = sizes
    half = width // 2
    lane = iota((1, LANES), 1)
    masks = [ones_where(lane < HEAD_DIM), ones_where(lane >= HEAD_DIM)]
    sums_q = jnp.zeros((1, half), F32)
    sums_v = jnp.zeros((1, half), F32)
    for row in range(2 * row_count):
        for place in range(half // LANES):
            cols = slice(place * LANES, (place + 1) * LANES)
            q_pair, k_pair, v_pair = query[row, :, cols], key[row, :, cols], value[row, :, cols]
            g_pair = gmixed[row, :, cols]
            found = []
            for sub in range(2):
                slope = slope_ref[2 * place + sub]
                scores = nt_dot(k_pair, q_pair * masks[sub]) - slope * dmt[row]
                peak = jnp.max(scores, axis=0, keepdims=True)
                raised = jnp.exp(scores - peak)
                exact = raised * (1.0 / jnp.sum(raised, axis=0, keepdims=True))
                gprobs = nt_dot(v_pair, g_pair * masks[sub])
                mean = jnp.sum(exact * gprobs, axis=0, keepdims=True)
                gscores = (exact * (gprobs - mean)).astype(BF16)
                found.append(
                    (
                        nn_dot(exact.astype(BF16), g_pair),
                        nn_dot(gscores, q_pair),
                        tn_dot(gscores, k_pair) * 0.125,
                    )
                )
            gvalue, gkey, gquery = (
                jnp.where(lane < HEAD_DIM, a, b).astype(BF16) for a, b in zip(found[0], found[1])
            )
            gv_out[row, :, cols] = gvalue
            gk_out[row, :, cols] = gkey
            gq_out[row * half_length : (row + 1) * half_length, cols] = gquery
        sums_q += jnp.sum(gq_out[row * half_length : (row + 1) * half_length, :].astype(F32), axis=0, keepdims=True)
        sums_v += jnp.sum(gv_out[row].astype(F32), axis=0, keepdims=True)
    heads_out[...] = jnp.concatenate([sums_q, sums_v, jnp.zeros((6, half), F32)], axis=0)


def attend_weight_kernel(
    sizes, core_ref, moved, pooled_low, spread, gq, gk, gv, mixed, gbranch, sums_one, sums_two, heads, gbup,
    heads_out, rest_out, send_out,
):
    row_count, seq_length, half_length, width, ff_half, per_up = sizes
    half = width // 2
    core = core_ref[0]
    heads_out[:, :half] = tn_dot(pooled_low[...], gq[...])
    for index, grad in ((1, gk), (2, gv)):
        total = None
        for row in range(2 * row_count):
            term = tn_dot(moved[row], grad[row])
            total = term if total is None else total + term
        heads_out[:, index * half : (index + 1) * half] = total
    per_chip = width // 16
    for chip in range(16):
        rows = slice(chip * per_chip + per_chip // 2, (chip + 1) * per_chip)
        send_out[chip] = heads_out[rows, :].astype(BF16)
    total = None
    for row in range(2 * row_count):
        term = tn_dot(mixed[row], gbranch[row * half_length : (row + 1) * half_length, :])
        total = term if total is None else total + term
    rest_out[:, :width] = total
    mine = [jnp.where(core == 0, sums[:, :half], sums[:, half:]) for sums in (sums_one, sums_two)]
    per_row = half * per_up // ff_half
    which = (iota((8, ff_half), 1) % per_up) // per_row
    high, low = two_parts(jnp.where(iota((8, ff_half), 0) == which, gbup[...], 0.0))
    ups = nt_dot(high, spread[...]) + nt_dot(low, spread[...])
    stacked = jnp.concatenate(
        [
            heads[0:2], mine[0][2:3], mine[0][0:2], mine[1][2:3], mine[1][0:2], ups,
            jnp.zeros((LANES - 16, half), F32),
        ],
        axis=0,
    )
    rest_out[:, width:] = stacked.T


def merge_kernel(core_ref, chip_ref, turn_ref, heads, rest, received, send_one, keep_one, send_two, keep_two):
    core = core_ref[0]
    width = heads.shape[0]
    half = width // 2
    per_row = width // 32
    own = pl.multiple_of(core * half, LANES)
    theirs = pl.multiple_of((1 - core) * half, LANES)
    for m in range(4):
        up, across = divmod(m, 2)
        one, one_at = (send_one, up) if across else (keep_one, up)
        two, two_at = (send_two, across) if up else (keep_two, across)
        for z in range(4):
            chip = 4 * m + turn_ref[z]
            mine = heads[pl.ds(pl.multiple_of(chip * 2 * per_row, 8), per_row), :]
            got = received[chip].astype(F32)
            place = pl.multiple_of(chip_ref[4 * m + z] * per_row, 8)
            outer = rest[pl.ds(place, per_row), :]
            for out, at, index, base in ((one, one_at, 0, 0), (one, one_at, 1, width), (two, two_at, 2, 0)):
                columns = slice(index * half, (index + 1) * half)
                out[at, z, :, pl.ds(base + own, half)] = mine[:, columns].astype(out.dtype)
                out[at, z, :, pl.ds(base + theirs, half)] = got[:, columns].astype(out.dtype)
            one[one_at, z, :, 2 * width :] = outer[:, width:].astype(one.dtype)
            two[two_at, z, :, width:] = outer[:, :width].astype(two.dtype)


def finish_kernel(mine_one, mine_two, first, second, third, q_out, k_out, v_out, o_out, *vectors):
    width = q_out.shape[1]
    per_row = q_out.shape[0]
    split = mine_one.shape[1]

    def total(own, start, size, base):
        terms = [a[:, base + start : base + start + size].astype(F32) for a in (first, second, third)]
        return own[:, start : start + size] + (terms[0] + (terms[1] + terms[2]))

    q_out[...] = total(mine_one, 0, width, 0)
    k_out[...] = total(mine_one, width, width, 0)
    v_out[...] = total(mine_two, 0, width, split)
    o_out[...] = total(mine_two, width, width, split)
    high, low = two_parts(total(mine_one, 2 * width, LANES, 0))
    eye = ones_where(iota((16, LANES), 0) == iota((16, LANES), 1))
    table = nt_dot(eye, high) + nt_dot(eye, low)
    for index in range(8):
        vectors[index][...] = table[index : index + 1, :]
    wide = vectors[8].shape[1]
    high, low = two_parts(table)
    fold = ones_where(iota((per_row, wide), 1) % per_row == iota((per_row, wide), 0))
    spread = nn_dot(high, fold) + nn_dot(low, fold)
    shape = (16, wide)
    picked = jnp.where(iota(shape, 0) == COL_BU + iota(shape, 1) // per_row, spread, 0.0)
    vectors[8][...] = jnp.sum(picked, axis=0, keepdims=True)


def input_grad(sizes, row, gq, gk, gv, wa, perm, extra):
    row_count, seq_length, half_length, width, ff_half, per_up = sizes
    half = width // 2
    grad = nt_dot(gk[row], wa[:, half:width]) + nt_dot(gv[row], wa[:, width:])
    high, low = two_parts(nt_dot(gq[row * half_length : (row + 1) * half_length, :], wa[:, :half]))
    shape = (seq_length, half_length)
    split = jnp.where(iota(shape, 0) // 2 == iota(shape, 1), 0.5, 0.0).astype(BF16)
    grad = grad + (nn_dot(split, high) + nn_dot(split, low))
    if extra is None:
        return nt_dot(grad.astype(BF16), perm[...])
    high, low = two_parts(grad)
    grad = nt_dot(high, perm[...]) + nt_dot(low, perm[...])
    high, low = two_parts(extra)
    return grad + (nn_dot(split, high) + nn_dot(split, low))


def other_inputs_kernel(sizes, gq, gk, gv, wa, perm, send_out):
    row_count, seq_length = sizes[0], sizes[1]
    for local in range(row_count):
        grad = input_grad(sizes, row_count + local, gq, gk, gv, wa, perm, None)
        send_out[local * seq_length : (local + 1) * seq_length, :] = grad.astype(BF16)


def own_inputs_kernel(sizes, gq, gk, gv, wa, perm, gh1, received, grad_out):
    row_count, seq_length, half_length = sizes[0], sizes[1], sizes[2]
    for local in range(row_count):
        extra = gh1[local * half_length : (local + 1) * half_length, :]
        grad = input_grad(sizes, local, gq, gk, gv, wa, perm, extra)
        rows = slice(local * seq_length, (local + 1) * seq_length)
        grad_out[rows, :] = grad + received[rows, :].astype(F32)


def run_kernel(kernel, outs, operands, scratch=(), scalars=0, weight=0.01, spare=8):
    specs = [pl.BlockSpec(memory_space=pltpu.SMEM)] * scalars
    specs += [pl.BlockSpec(memory_space=pltpu.VMEM)] * (len(operands) - scalars)
    moved = sum(a.size * a.dtype.itemsize for a in list(operands) + list(outs))
    held = sum(math.prod(a.shape) * 4 for a in scratch)
    return pl.pallas_call(
        kernel,
        out_shape=tuple(outs),
        in_specs=specs,
        out_specs=tuple(pl.BlockSpec(memory_space=pltpu.VMEM) for _ in outs),
        scratch_shapes=list(scratch),
        compiler_params=pltpu.CompilerParams(vmem_limit_bytes=int(moved * 1.05) + held + spare * MIB),
        cost_estimate=pl.CostEstimate(flops=int(weight * 1e9), bytes_accessed=int(weight * 1e6), transcendentals=0),
    )(*operands)


def shape_of(shape, dtype):
    return jax.ShapeDtypeStruct(shape, dtype)


def shift(array, step):
    return lax.ppermute(array, "fsdp", [(i, i ^ (4 * step)) for i in range(16)])


def swap(array, bit):
    return lax.ppermute(array, "fsdp", [(i, i ^ bit) for i in range(16)])


def gather_z(pack):
    return [pack] + [shift(pack, step) for step in (1, 2, 3)]


def onward(array, step):
    return lax.ppermute(array, "fsdp", [(i, (i + 4 * step) % 16) for i in range(16)])


def pair_z(pack):
    return jnp.stack([pack, shift(pack, 2)], axis=0)


def column_of(pair, rest, part):
    return jnp.concatenate([pair[0, part], rest[0, part], pair[1, part], rest[1, part]], axis=0)


def near_pieces(one, two):
    return jnp.stack([one, swap(one, 1)], axis=0), jnp.stack([two, swap(two, 2)], axis=0)


def far_pieces(one_near, two_near):
    return swap(one_near, 2), swap(two_near, 1)


def all_pieces(near, far):
    return near[0], far[0], near[1], far[1]


def after(arrays, others):
    return lax.optimization_barrier((arrays, others))[0]


def scatter_near(blocks):
    return swap(blocks[0], 1), swap(blocks[2], 2)


def scatter_far(blocks, got):
    keep_one, keep_two = blocks[1], blocks[3]
    got_one, got_two = got
    next_one = (keep_one[1] + got_one[1].astype(F32)).astype(BF16)
    next_two = (keep_two[1] + got_two[1].astype(F32)).astype(BF16)
    last_one, last_two = swap(next_one, 2), swap(next_two, 1)
    one = keep_one[0] + got_one[0].astype(F32) + last_one.astype(F32)
    two = keep_two[0] + got_two[0].astype(F32) + last_two.astype(F32)
    return one, two


def send_z(parts):
    rows = [a.shape[0] // 4 for a in parts]
    axis = 0 if len({a.shape for a in parts}) == 1 else -1
    received = []
    for step in (1, 2, 3):
        blocks = [a[step * n : (step + 1) * n].astype(BF16) for a, n in zip(parts, rows)]
        received.append(onward(jnp.concatenate(blocks, axis=axis), step))
    return [a[:n] for a, n in zip(parts, rows)], received


def sum_z(mine, received):
    axis = 0 if len({a.shape for a in mine}) == 1 else -1
    ends = [0]
    for block in mine:
        ends.append(ends[-1] + block.shape[axis])
    return [
        block + sum(lax.slice_in_dim(got, start, end, axis=axis).astype(F32) for got in received)
        for block, start, end in zip(mine, ends, ends[1:])
    ]


def half_columns(array, which):
    size = array.shape[1] // 2
    return lax.dynamic_slice_in_dim(array, which * size, size, axis=1)


def halves(array):
    size = array.shape[1] // 2
    return [array[:, :size], array[:, size:]]


def as_pieces(one, two):
    one, two = (a.reshape((4, a.shape[0] // 4) + a.shape[1:]) for a in (one, two))
    return one[:2], one[2:], two[0::2], two[1::2]


def gather_flat(core, weights):
    w_q, w_k, w_v, w_o, biases, w_up, w_down = (lax.all_gather(w, AXES, axis=0, tiled=True) for w in weights)
    width = w_q.shape[0]
    half = width // 2
    wo = jnp.concatenate(halves(lax.dynamic_slice_in_dim(w_o, core * half, half)), axis=0)
    q, k, v = (half_columns(w, core) for w in (w_q, w_k, w_v))
    pieces_a = as_pieces(jnp.concatenate([q, k, biases], axis=1), jnp.concatenate([v, wo], axis=1))
    up = halves(half_columns(w_up, core))
    ff_half = w_down.shape[0] // 2
    down = lax.dynamic_slice_in_dim(w_down, core * ff_half, ff_half).reshape(16, 2, -1, width)
    return pieces_a, as_pieces(*up), as_pieces(*(down[:, part].reshape(-1, width) for part in range(2)))


def scatter_rows(array):
    return lax.psum_scatter(array, AXES, scatter_dimension=0, tiled=True)


def placed(array, core, axis):
    shape = list(array.shape)
    shape[axis] *= 2
    return lax.dynamic_update_slice_in_dim(jnp.zeros(shape, array.dtype), array, core * array.shape[axis], axis)


def whole_of(blocks):
    send_one, keep_one, send_two, keep_two = (a.astype(F32) for a in blocks)
    one = jnp.stack([keep_one, send_one], axis=1)
    two = jnp.stack([keep_two, send_two], axis=0)
    return [a.reshape((-1,) + a.shape[3:]) for a in (one, two)]


def scatter_ffn_flat(core, up_blocks, down_blocks):
    up = placed(jnp.concatenate(whole_of(up_blocks), axis=1), core, 1)
    one, two = whole_of(down_blocks)
    width = one.shape[1]
    down = jnp.stack([one.reshape(16, -1, width), two.reshape(16, -1, width)], axis=1).reshape(-1, width)
    return scatter_rows(up), scatter_rows(placed(down, core, 0))


def scatter_attention_flat(core, heads, rest):
    width = heads.shape[0]
    half = width // 2
    found = [scatter_rows(placed(heads[:, i * half : (i + 1) * half], core, 1)) for i in range(3)]
    return found + [scatter_rows(placed(a, core, 0)) for a in (rest[:, :width], rest[:, width:])]


def body(mesh_shape, *args):
    (
        inputs, segments, w_q, b_q, w_k, w_v, b_v, w_o, b_o, ln1_gain, ln1_bias, w_up, b_up, w_down,
        b_down, ln2_gain, ln2_bias, grad_out,
    ) = args
    dp_size, fsdp_size = mesh_shape
    by_chips = (dp_size, fsdp_size) == (2, 16)
    row_count, seq_length, width = inputs.shape
    half_length = seq_length // 2
    half = width // 2
    per_row, ff = w_up.shape
    ff_half = ff // 2
    per_up = w_down.shape[0]
    ratio = per_up // per_row
    rows2 = 2 * row_count
    tokens = rows2 * half_length
    core = lax.axis_index("dp") & 1
    core_at = core.reshape(1).astype(jnp.int32)
    heads = width // HEAD_DIM
    slopes = 2.0 ** (-8.0 * (jnp.arange(heads, dtype=F32) + 1.0) / heads)
    slopes = jnp.where(core == 0, slopes[: heads // 2], slopes[heads // 2 :])
    swap_pairs = [(i, i ^ 1) for i in range(dp_size)]

    def swap_cores(array):
        return lax.ppermute(array, "dp", swap_pairs)

    place = jnp.arange(width, dtype=jnp.int32)
    if by_chips:
        index = lax.axis_index("fsdp")
        z, yx = index >> 2, index & 3
        m, s = place // (width // 4), place // (width // 16) % 4
        chip = 4 * (z ^ s) + (yx ^ m)
        order = (core ^ (place // per_row % 2)) * half + chip * per_row + place % per_row
        number = jnp.arange(16, dtype=jnp.int32)
        chip_at = 4 * (z ^ (number & 3)) + (yx ^ (number // 4))
        chip_to = 4 * ((z + number) & 3) + (yx ^ (number // 4))
        turn = z ^ ((z + number[:4]) & 3)
        spread_rows = per_up
    else:
        order, chip_at, spread_rows = place, jnp.arange(16, dtype=jnp.int32), per_up
        chip_to, turn = chip_at, chip_at[:4]
    sizes = (row_count, seq_length, half_length, width, ff_half, spread_rows)
    order = jnp.broadcast_to(order, (8, width)).astype(jnp.int32)

    vectors = (b_q, b_v, b_o, ln1_gain, ln1_bias, b_down, ln2_gain, ln2_bias)
    seg_rows = jnp.pad(segments.astype(BF16), ((0, 16 - row_count), (0, width - seq_length)))
    act_own = jnp.concatenate(
        [inputs.reshape(-1, width), grad_out.reshape(-1, width), seg_rows], axis=0
    )
    act_other = swap_cores(act_own)

    def prepare(acts):
        return run_kernel(
            functools.partial(ready_kernel, sizes),
            [
                shape_of((width, width), BF16),
                shape_of((rows2, seq_length, width), BF16),
                shape_of((tokens, width), F32),
                shape_of((tokens, width), BF16),
                shape_of((rows2, half_length, seq_length), F32),
                shape_of((rows2, seq_length, half_length), F32),
                shape_of((half, ff_half), BF16),
            ],
            [order, *acts],
            weight=20,
        )

    if by_chips:
        base = width + LANES + half
        send, own, own_up = run_kernel(
            pack_kernel,
            [shape_of((per_row, base + ff_half), BF16), shape_of((per_row, base), BF16), shape_of((per_row, ff_half), BF16)],
            [core_at, w_q, w_k, w_v, w_up, b_up.reshape(1, -1)] + [v.reshape(1, -1) for v in vectors],
            scalars=1,
            spare=54,
        )
        received = swap_cores(send)
        pack_a, pack_up = run_kernel(
            chip_pack_kernel,
            [shape_of((2, per_row, base + half), BF16), shape_of((2, 2, per_row, width), BF16)],
            [core_at, own, received, own_up, w_o],
            scalars=1,
            spare=54,
        )
        pack_up = pack_up.reshape(2, 2 * per_row, width)
        pack_down = w_down.reshape(2, 2 * per_row, width)
        around = gather_z(after(pack_a, act_other).reshape(2 * per_row, base + half))
        split = width + LANES
        one = jnp.concatenate([a[:, :split] for a in around], axis=0)
        two = jnp.concatenate([a[:, split:] for a in around], axis=0)
        near_a = near_pieces(one, two)
        up_pair = pair_z(after(pack_up, (one, two)))
        far_a = far_pieces(*near_a)
        up_pair = after(up_pair, near_a)
        up_rest = shift(up_pair, 1)
        down_pair = pair_z(after(pack_down, up_pair))
        perm, *prepared = prepare(after((act_own, act_other), (near_a, up_pair)))
        up_pair, up_rest = after((up_pair, up_rest), (perm, far_a))
        ups = [column_of(up_pair, up_rest, part) for part in range(2)]
        near_up = near_pieces(*ups)
        pieces_a = all_pieces(near_a, after(far_a, ups))
        down_pair = after(down_pair, ups)
        down_rest = shift(down_pair, 1)
    else:
        biases = jnp.stack(vectors, axis=0)
        biases = jnp.concatenate([biases, b_up.reshape(ratio, per_row)], axis=0)
        biases = jnp.pad(biases, ((0, LANES - 8 - ratio), (0, 0))).T
        perm, *prepared = prepare((act_own, act_other))
        near_up, (pieces_a, pieces_up, pieces_down) = (), gather_flat(core, (w_q, w_k, w_v, w_o, biases, w_up, w_down))
    moved, pooled, pooled_low, dm, dmt, spread = prepared
    q_rows, k_rows, v_rows, wa, wo_own, table, bup = run_kernel(
        functools.partial(project_kernel, sizes),
        [
            shape_of((rows2, half_length, half), BF16),
            shape_of((rows2, seq_length, half), BF16),
            shape_of((rows2, seq_length, half), BF16),
            shape_of((width, 3 * half), BF16),
            shape_of((2, half, half), BF16),
            shape_of((16, width), F32),
            shape_of((8, ff_half), F32),
        ],
        [core_at, moved, pooled_low, perm, spread, *pieces_a],
        [pltpu.VMEM((width, half), BF16), pltpu.VMEM((width, LANES), BF16)],
        scalars=1,
    )
    if by_chips:
        near_up = after(near_up, q_rows)
        downs = [column_of(*after((down_pair, down_rest), near_up), part) for part in range(2)]
        near_down = near_pieces(*downs)
        pieces_up = all_pieces(near_up, far_pieces(*near_up))
        pieces_down = all_pieces(near_down, far_pieces(*near_down))
        q_rows = after(q_rows, near_down)
    (mixed,) = run_kernel(
        functools.partial(attend_kernel, sizes),
        [shape_of((rows2, half_length, half), BF16)],
        [slopes, dm, q_rows, k_rows, v_rows],
        scalars=1,
    )
    wo_other = swap_cores(wo_own)
    mixed_other = swap_cores(mixed)
    normed_one, inverse_one, first_low, active, bend, up = run_kernel(
        functools.partial(ffn_up_kernel, sizes),
        [
            shape_of((tokens, width), F32),
            shape_of((tokens, LANES), F32),
            shape_of((tokens, width), BF16),
            shape_of((tokens, ff_half), BF16),
            shape_of((tokens, ff_half), F32),
            shape_of((2, width, width), BF16),
        ],
        [pooled, mixed, mixed_other, wo_own, wo_other, table, bup, perm, *pieces_up],
    )
    part_two, down = run_kernel(
        functools.partial(ffn_down_kernel, sizes),
        [shape_of((tokens, width), BF16), shape_of((ff_half, width), BF16)],
        [chip_at, active, *pieces_down],
        scalars=1,
    )
    part_other = swap_cores(part_two)
    block = width // 4
    send_shape, keep_shape = shape_of((2, block, width), BF16), shape_of((2, block, width), F32)
    output, gh2, gsec, sums_two, *down_blocks = run_kernel(
        functools.partial(second_norm_kernel, sizes),
        [
            shape_of((row_count * half_length, width), BF16),
            shape_of((tokens, width), F32),
            shape_of((tokens, width), BF16),
            shape_of((8, width), F32),
            send_shape, keep_shape, send_shape, keep_shape,
        ],
        [chip_to, act_own, act_other, normed_one, part_two, part_other, table, active],
        [pltpu.VMEM((ff_half, width), F32)],
        scalars=1,
    )
    ginner, gfirst, gbup = run_kernel(
        functools.partial(ffn_back_kernel, sizes),
        [shape_of((tokens, ff_half), BF16), shape_of((tokens, width), BF16), shape_of((8, ff_half), F32)],
        [gsec, bend, perm, up, down],
    )
    gfirst_other = swap_cores(gfirst)
    up_blocks = run_kernel(
        ffn_weight_kernel,
        [send_shape, keep_shape, send_shape, keep_shape],
        [turn, first_low, ginner],
        [pltpu.VMEM((width, width), F32)],
        scalars=1,
    )
    gh1, gbranch, gmixed, sums_one = run_kernel(
        functools.partial(first_norm_kernel, sizes),
        [
            shape_of((row_count * half_length, width), F32),
            shape_of((tokens, width), BF16),
            shape_of((rows2, half_length, half), BF16),
            shape_of((8, width), F32),
        ],
        [normed_one, inverse_one, gh2, gfirst, after(gfirst_other, tuple(up_blocks)), table, wo_own],
    )
    gq, gk, gv, head_sums = run_kernel(
        functools.partial(attend_back_kernel, sizes),
        [
            shape_of((tokens, half), BF16),
            shape_of((rows2, seq_length, half), BF16),
            shape_of((rows2, seq_length, half), BF16),
            shape_of((8, half), F32),
        ],
        [slopes, dmt, gmixed, q_rows, k_rows, v_rows],
        scalars=1,
    )
    grad_heads, grad_rest, heads_send = run_kernel(
        functools.partial(attend_weight_kernel, sizes),
        [
            shape_of((width, 3 * half), F32),
            shape_of((half, width + LANES), F32),
            shape_of((16, width // 32, 3 * half), BF16),
        ],
        [core_at, moved, pooled_low, spread, gq, gk, gv, mixed, gbranch, sums_one, sums_two, head_sums, gbup],
        scalars=1,
    )
    if by_chips:
        down_parts = scatter_far(down_blocks, after(scatter_near(down_blocks), gq))
        heads_other = swap_cores(heads_send)
        got_up = after(scatter_near(up_blocks), heads_send)
        grad_heads = after(grad_heads, got_up)
        blocks = (4, per_row)
        columns_one, columns_two = 2 * width + LANES, 2 * width
        attend_blocks = run_kernel(
            merge_kernel,
            [
                shape_of((2,) + blocks + (columns_one,), BF16),
                shape_of((2,) + blocks + (columns_one,), F32),
                shape_of((2,) + blocks + (columns_two,), BF16),
                shape_of((2,) + blocks + (columns_two,), F32),
            ],
            [core_at, chip_to, turn, grad_heads, grad_rest, heads_other],
            scalars=3,
        )
        attend_blocks = after(tuple(attend_blocks), down_parts)
        up_parts = scatter_far(up_blocks, got_up)
        got_attend = scatter_near(attend_blocks)
        gq = after(gq, up_parts)
    (inputs_send,) = run_kernel(
        functools.partial(other_inputs_kernel, sizes),
        [shape_of((row_count * seq_length, width), BF16)],
        [gq, gk, gv, wa, perm],
    )
    if by_chips:
        parts_f, z_blocks = send_z([*down_parts, *up_parts])
        parts_a = scatter_far(attend_blocks, got_attend)
        inputs_send = after(inputs_send, parts_a)
    inputs_other = swap_cores(inputs_send)
    (grad_inputs,) = run_kernel(
        functools.partial(own_inputs_kernel, sizes),
        [shape_of((row_count * seq_length, width), F32)],
        [gq, gk, gv, wa, perm, gh1, inputs_other],
    )
    if by_chips:
        z_blocks = after(z_blocks, parts_a)
        down_one, down_two, up_one, up_two = sum_z(parts_f, z_blocks)
        grad_down = jnp.concatenate([down_one, down_two], axis=0)
        up_got = swap_cores(jnp.concatenate([up_one[per_row:], up_two[per_row:]], axis=1))
        up_mine = jnp.concatenate([up_one[:per_row], up_two[:per_row]], axis=1)
        grad_up = jnp.where(
            core == 0, jnp.concatenate([up_mine, up_got], -1), jnp.concatenate([up_got, up_mine], -1)
        )
        mine, received = send_z(list(parts_a))
        received = after(received, (grad_inputs, grad_up, grad_down))
        square, vector = shape_of((per_row, width), F32), shape_of((1, per_row), F32)
        found = run_kernel(
            finish_kernel,
            [square] * 4 + [vector] * 8 + [shape_of((1, per_up), F32)],
            [a.reshape(per_row, -1) for a in (*mine, *received)],
        )
        grad_q, grad_k, grad_v, grad_o = found[:4]
        g_bq, g_bv, g_bo, g_g1, g_s1, g_bd, g_g2, g_s2, g_bu = (a.reshape(-1) for a in found[4:])
    else:
        grad_up, grad_down = scatter_ffn_flat(core, up_blocks, down_blocks)
        found = scatter_attention_flat(core, grad_heads, grad_rest)
        grad_q, grad_k, grad_v, grad_o = found[:4]
        small = found[4].T
        g_bq, g_bv, g_bo, g_g1, g_s1, g_bd, g_g2, g_s2 = (small[i] for i in range(8))
        g_bu = small[8 : 8 + ratio].reshape(per_up)
    return (
        output.reshape(row_count, half_length, width),
        grad_inputs.reshape(row_count, seq_length, width),
        grad_q, g_bq, grad_k, grad_v, g_bv, grad_o, g_bo, g_g1, g_s1, grad_up, g_bu, grad_down, g_bd, g_g2, g_s2,
    )


def solution(mesh):
    rows, matrix, vector = P(AXES, None, None), P(AXES, None), P(AXES)
    in_specs = (
        rows, matrix, matrix, vector, matrix, matrix, vector, matrix, vector, vector, vector, matrix, vector,
        matrix, vector, vector, vector, rows,
    )
    out_specs = (
        rows, rows, matrix, vector, matrix, matrix, vector, matrix, vector, vector, vector, matrix, vector,
        matrix, vector, vector, vector,
    )
    shape = (mesh.shape["dp"], mesh.shape["fsdp"])
    return jax.shard_map(
        functools.partial(body, shape), mesh=mesh, in_specs=in_specs, out_specs=out_specs, check_vma=False
    )
```

```python
import functools
import math

import jax
import jax.numpy as jnp
from jax import lax
from jax.experimental import pallas as pl
from jax.experimental.pallas import tpu as pltpu
from jax.sharding import PartitionSpec as P

HEAD_DIM = 64
LANES = 128
EPSILON = 1e-06
FAR = 1e12
AXES = ("dp", "fsdp")
BF16 = jnp.bfloat16
F32 = jnp.float32
MIB = 1024 * 1024


def nn_dot(left, right):
    return jnp.dot(left, right, preferred_element_type=F32)


def nt_dot(left, right):
    return lax.dot_general(left, right, (((1,), (1,)), ((), ())), preferred_element_type=F32)


def tn_dot(left, right):
    return lax.dot_general(left, right, (((0,), (0,)), ((), ())), preferred_element_type=F32)


def iota(shape, axis):
    return lax.broadcasted_iota(jnp.int32, shape, axis)


def ones_where(condition):
    return jnp.where(condition, 1.0, 0.0).astype(BF16)


def two_parts(array):
    high = array.astype(BF16)
    return high, (array - high.astype(F32)).astype(BF16)


def mean_of(array):
    return jnp.mean(array, axis=-1, keepdims=True)


def gelu_parts(value):
    scale = 0.7978845608028654
    square = value * value
    bend = jnp.tanh(scale * value * (1.0 + 0.044715 * square))
    half = 0.5 * (1.0 + bend)
    slope = half + 0.5 * value * (1.0 - bend * bend) * scale * (1.0 + 3.0 * 0.044715 * square)
    return value * half, slope


COL_BQ, COL_BV, COL_BO, COL_G1, COL_S1, COL_BD, COL_G2, COL_S2, COL_BU = 0, 1, 2, 3, 4, 5, 6, 7, 8


def up_spread(half, ff_half, per_up):
    rows = iota((half, ff_half), 0)
    cols = iota((half, ff_half), 1)
    per_row = half * per_up // ff_half
    same_chip = rows // per_row == cols // per_up
    same_place = rows % per_row == cols % per_row
    return ones_where(same_chip & same_place)


def pack_kernel(core_ref, w_q, w_k, w_v, w_up, b_up, *refs):
    vectors, send_out, own_out, up_out = refs[:8], refs[8], refs[9], refs[10]
    core = core_ref[0]
    per_row, width = w_q.shape
    half = width // 2
    ff_half = w_up.shape[1] // 2
    count = b_up.shape[1]
    table = jnp.concatenate([v[...].astype(F32) for v in vectors] + [jnp.zeros((LANES - 8, per_row), F32)], axis=0)
    eye = ones_where(iota((per_row, per_row), 0) == iota((per_row, per_row), 1))
    shape = (LANES, count)
    spread = jnp.where(iota(shape, 1) // per_row + COL_BU == iota(shape, 0), b_up[...].astype(F32), 0.0)
    fold = ones_where(iota((per_row, count), 1) % per_row == iota((per_row, count), 0))
    biases = (nt_dot(eye, table.astype(BF16)) + nt_dot(fold, spread.astype(BF16))).astype(BF16)
    for out, which in ((send_out, 1 - core), (own_out, core)):
        start = pl.multiple_of(which * half, LANES)
        out[:, :half] = w_q[:, pl.ds(start, half)]
        out[:, half : 2 * half] = w_k[:, pl.ds(start, half)]
        out[:, width : width + LANES] = biases
        out[:, width + LANES : width + LANES + half] = w_v[:, pl.ds(start, half)]
    up_start = pl.multiple_of(core * ff_half, LANES)
    other_start = pl.multiple_of((1 - core) * ff_half, LANES)
    up_out[...] = w_up[:, pl.ds(up_start, ff_half)]
    send_out[:, width + LANES + half :] = w_up[:, pl.ds(other_start, ff_half)]


def chip_pack_kernel(core_ref, own, received, own_up, w_o, pack_a, pack_up):
    core = core_ref[0]
    width = w_o.shape[1]
    half = width // 2
    base = width + LANES + half
    pack_a[0, :, :base] = own[...]
    pack_a[1, :, :base] = received[:, :base]
    for place, which in ((0, core), (1, 1 - core)):
        start = pl.multiple_of(which * half, LANES)
        pack_a[place, :, base:] = w_o[:, pl.ds(start, half)]
    for part in range(2):
        pack_up[part, 0] = own_up[:, part * width : (part + 1) * width]
        pack_up[part, 1] = received[:, base + part * width : base + (part + 1) * width]


def ready_kernel(sizes, order, act_own, act_other, perm_out, moved_out, pooled_out, pooled_low_out, dm_out, dmt_out, spread_out):
    row_count, seq_length, half_length, width, ff_half, per_up = sizes
    perm_out[...] = ones_where(iota((width, width), 0) == order[0:1, :])
    spread_out[...] = up_spread(width // 2, ff_half, per_up)
    shape, turned = (half_length, seq_length), (seq_length, half_length)
    pool = jnp.where(iota(shape, 1) // 2 == iota(shape, 0), 0.5, 0.0).astype(BF16)
    evens = ones_where(iota(shape, 1) == 2 * iota(shape, 0))
    eye = ones_where(iota((seq_length, seq_length), 0) == iota((seq_length, seq_length), 1))
    distance = jnp.abs((iota(shape, 1) - 2 * iota(shape, 0)).astype(F32) - 0.5)
    distance_t = jnp.abs((iota(turned, 0) - 2 * iota(turned, 1)).astype(F32) - 0.5)
    base = row_count * (seq_length + half_length)
    for row in range(2 * row_count):
        act = act_own if row < row_count else act_other
        local = row % row_count
        hidden = act[local * seq_length : (local + 1) * seq_length, :]
        rows = slice(row * half_length, (row + 1) * half_length)
        pooled = nn_dot(pool, hidden)
        pooled_out[rows, :] = pooled
        pooled_low_out[rows, :] = nn_dot(pooled.astype(BF16), perm_out[...]).astype(BF16)
        moved_out[row] = nn_dot(hidden, perm_out[...]).astype(BF16)
        seg_rows = act[base : base + 16, :seq_length]
        here = slice(local, local + 1)
        seg_query = nt_dot(evens, seg_rows)[:, here]
        dm_out[row] = jnp.where(seg_query == seg_rows[here].astype(F32), distance, FAR)
        seg_key = nt_dot(eye, seg_rows)[:, here]
        dmt_out[row] = jnp.where(seg_key == nt_dot(seg_rows, evens)[here, :], distance_t, FAR)


def pieces_of(one_near, one_far, two_near, two_far, m):
    up, across = divmod(m, 2)
    return (one_near, one_far)[up].at[across], (two_near, two_far)[across].at[up]


def project_kernel(
    sizes, core_ref, moved, pooled_low, perm, spread, one_near, one_far, two_near, two_far,
    q_out, k_out, v_out, wa_out, wo_out, table_out, bup_out, wo_perm, bias_perm,
):
    row_count, seq_length, half_length, width, ff_half, per_up = sizes
    half = width // 2
    block = width // 4
    core = core_ref[0]
    for m in range(4):
        one, two = pieces_of(one_near, one_far, two_near, two_far, m)
        rows = slice(m * block, (m + 1) * block)
        wa_out[rows, :width] = one[:, :width]
        bias_perm[rows, :] = one[:, width:]
        wa_out[rows, width:] = two[:, :half]
        wo_perm[rows, :] = two[:, half:]
    eye = ones_where(iota((16, LANES), 0) == iota((16, LANES), 1))
    table = nt_dot(nt_dot(eye, bias_perm[...]).astype(BF16), perm[...])
    table_out[...] = table
    mine = jnp.where(core == 0, table[:, :half], table[:, half:])
    ups = nn_dot(mine.astype(BF16), spread[...])
    per_row = half * per_up // ff_half
    which = (iota((16, ff_half), 1) % per_up) // per_row + COL_BU
    bup = jnp.sum(jnp.where(iota((16, ff_half), 0) == which, ups, 0.0), axis=0, keepdims=True)
    bup_out[...] = jnp.broadcast_to(bup, (8, ff_half))
    bias_q, bias_v = mine[COL_BQ : COL_BQ + 1], mine[COL_BV : COL_BV + 1]
    for row in range(2 * row_count):
        rows = slice(row * half_length, (row + 1) * half_length)
        query = nn_dot(pooled_low[rows, :], wa_out[:, :half]) + bias_q
        q_out[row] = (query.astype(BF16).astype(F32) * 0.125).astype(BF16)
        k_out[row] = nn_dot(moved[row], wa_out[:, half:width]).astype(BF16)
        v_out[row] = (nn_dot(moved[row], wa_out[:, width:]) + bias_v).astype(BF16)
    for side in range(2):
        wo_out[side] = nn_dot(perm[side * half : (side + 1) * half, :], wo_perm[...]).astype(BF16)


def attend_kernel(sizes, slope_ref, dm, query, key, value, mixed_out):
    row_count, seq_length, half_length, width, ff_half, per_up = sizes
    lane = iota((1, LANES), 1)
    masks = [ones_where(lane < HEAD_DIM), ones_where(lane >= HEAD_DIM)]
    for row in range(2 * row_count):
        for place in range(width // 2 // LANES):
            cols = slice(place * LANES, (place + 1) * LANES)
            q_pair, k_pair, v_pair = query[row, :, cols], key[row, :, cols], value[row, :, cols]
            results = []
            for sub in range(2):
                slope = slope_ref[2 * place + sub]
                scores = nt_dot(q_pair * masks[sub], k_pair) - slope * dm[row]
                peak = jnp.max(scores, axis=-1, keepdims=True)
                raised = jnp.exp(scores - peak)
                total = jnp.sum(raised, axis=-1, keepdims=True)
                probs = (raised * (1.0 / total)).astype(BF16)
                results.append(nn_dot(probs, v_pair))
            mixed_out[row, :, cols] = jnp.where(lane < HEAD_DIM, results[0], results[1]).astype(BF16)


def ffn_up_kernel(
    sizes, pooled, mixed_own, mixed_other, wo_own, wo_other, table, bup, perm,
    one_near, one_far, two_near, two_far,
    normed_out, inverse_out, low_out, active_out, bend_out, up_out,
):
    row_count, seq_length, half_length, width, ff_half, per_up = sizes
    block = width // 4
    for m in range(4):
        for part, piece in enumerate(pieces_of(one_near, one_far, two_near, two_far, m)):
            up_out[part, m * block : (m + 1) * block, :] = piece[...]
    for row in range(2 * row_count):
        rows = slice(row * half_length, (row + 1) * half_length)
        own = mixed_own[row]
        other = mixed_other[(row + row_count) % (2 * row_count)]
        parts = [nn_dot(own, wo_own[side]) + nn_dot(other, wo_other[side]) for side in range(2)]
        hidden = pooled[rows, :] + (jnp.concatenate(parts, axis=1) + table[COL_BO : COL_BO + 1, :])
        center = hidden - mean_of(hidden)
        inverse = lax.rsqrt(mean_of(center * center) + EPSILON)
        normed = center * inverse
        normed_out[rows, :] = normed
        inverse_out[rows, :] = jnp.broadcast_to(inverse, (half_length, LANES))
        first = normed * table[COL_G1 : COL_G1 + 1, :] + table[COL_S1 : COL_S1 + 1, :]
        low_out[rows, :] = nn_dot(first.astype(BF16), perm[...]).astype(BF16)
    chunk = 256
    for start in range(0, ff_half, chunk):
        cols = slice(start, start + chunk)
        side, inside = divmod(start, width)
        inner = nn_dot(low_out[...], up_out[side, :, inside : inside + chunk]) + bup[0:1, cols]
        active, slope = gelu_parts(inner)
        active_out[:, cols] = active.astype(BF16)
        bend_out[:, cols] = slope


def ffn_down_kernel(sizes, chip_ref, active, one_near, one_far, two_near, two_far, send_out, down_out):
    width = sizes[3]
    per_z = width // 16
    for m in range(4):
        for part, piece in enumerate(pieces_of(one_near, one_far, two_near, two_far, m)):
            for z in range(4):
                place = chip_ref[4 * m + z] * (2 * per_z) + part * per_z
                down_out[pl.ds(pl.multiple_of(place, 16), per_z), :] = piece[z * per_z : (z + 1) * per_z, :]
    chunk = 256
    for start in range(0, width, chunk):
        cols = slice(start, start + chunk)
        send_out[:, cols] = nn_dot(active[...], down_out[:, cols]).astype(BF16)


def store_blocks(array, rows_of, part, send_out, keep_out, block):
    for m in range(4):
        up, across = divmod(m, 2)
        leaves, index = (across, up) if part == 0 else (up, across)
        for at, size, rows in rows_of(m):
            value = array[rows, :]
            if leaves:
                send_out[index, at : at + size, :] = value.astype(BF16)
            else:
                keep_out[index, at : at + size, :] = value


def second_norm_kernel(
    sizes, chip_ref, act_own, act_other, normed_one, part_own, part_other, table, active,
    out_out, gh2_out, gsec_out, sums_out, send_one, keep_one, send_two, keep_two, gdown,
):
    row_count, seq_length, half_length, width, ff_half, per_up = sizes
    gain_two = table[COL_G2 : COL_G2 + 1, :]
    zero = jnp.zeros((1, width), F32)
    sum_gain, sum_shift, sum_down = zero, zero, zero
    for row in range(2 * row_count):
        rows = slice(row * half_length, (row + 1) * half_length)
        swapped = (row + row_count) % (2 * row_count)
        other_rows = slice(swapped * half_length, (swapped + 1) * half_length)
        act = act_own if row < row_count else act_other
        base = row_count * seq_length + (row % row_count) * half_length
        first = normed_one[rows, :] * table[COL_G1 : COL_G1 + 1, :] + table[COL_S1 : COL_S1 + 1, :]
        second = part_own[rows, :].astype(F32) + part_other[other_rows, :].astype(F32)
        hidden = first + (second + table[COL_BD : COL_BD + 1, :])
        center = hidden - mean_of(hidden)
        inverse = lax.rsqrt(mean_of(center * center) + EPSILON)
        normed = center * inverse
        if row < row_count:
            out_out[rows, :] = (normed * gain_two + table[COL_S2 : COL_S2 + 1, :]).astype(BF16)
        upstream = act[base : base + half_length, :].astype(F32)
        sum_gain += jnp.sum(upstream * normed, axis=0, keepdims=True)
        sum_shift += jnp.sum(upstream, axis=0, keepdims=True)
        scaled = upstream * gain_two
        grad = inverse * (scaled - mean_of(scaled) - normed * mean_of(scaled * normed))
        gh2_out[rows, :] = grad
        low = grad.astype(BF16)
        gsec_out[rows, :] = low
        sum_down += jnp.sum(low.astype(F32), axis=0, keepdims=True)
    sums_out[...] = jnp.concatenate([sum_gain, sum_shift, sum_down, jnp.zeros((5, width), F32)], axis=0)
    chunk = 256
    for start in range(0, ff_half, chunk):
        gdown[start : start + chunk, :] = tn_dot(active[:, start : start + chunk], gsec_out[...])
    per_z = width // 16
    for part, send_out, keep_out in ((0, send_one, keep_one), (1, send_two, keep_two)):

        def rows_of(m, part=part):
            for z in range(4):
                place = chip_ref[4 * m + z] * (2 * per_z) + part * per_z
                yield z * per_z, per_z, pl.ds(pl.multiple_of(place, 16), per_z)

        store_blocks(gdown, rows_of, part, send_out, keep_out, width // 4)


def ffn_back_kernel(sizes, gsec, bend, perm, up, down, ginner_out, gfirst_out, gbup_out):
    row_count, seq_length, half_length, width, ff_half, per_up = sizes
    chunk = 256
    for start in range(0, ff_half, chunk):
        cols = slice(start, start + chunk)
        grad = (nt_dot(gsec[...], down[cols, :]) * bend[:, cols]).astype(BF16)
        ginner_out[:, cols] = grad
        total = jnp.sum(grad.astype(F32), axis=0, keepdims=True)
        gbup_out[:, cols] = jnp.broadcast_to(total, (8, chunk))
    part = nt_dot(ginner_out[:, :width], up[0]) + nt_dot(ginner_out[:, width:], up[1])
    gfirst_out[...] = nt_dot(part.astype(BF16), perm[...]).astype(BF16)


def ffn_weight_kernel(turn_ref, low, ginner, send_one, keep_one, send_two, keep_two, gup):
    width = low.shape[1]
    block = width // 4
    chunk = 256
    for part, send_out, keep_out in ((0, send_one, keep_one), (1, send_two, keep_two)):
        for start in range(0, width, chunk):
            gup[start : start + chunk, :] = tn_dot(
                low[:, start : start + chunk], ginner[:, part * width : (part + 1) * width]
            )

        def rows_of(m):
            per_z = block // 4
            for z in range(4):
                place = m * block + turn_ref[z] * per_z
                yield z * per_z, per_z, pl.ds(pl.multiple_of(place, 16), per_z)

        store_blocks(gup, rows_of, part, send_out, keep_out, block)


def first_norm_kernel(
    sizes, normed_one, inverse_one, gh2, gfirst_own, gfirst_other, table, wo_own,
    gh1_out, gbranch_out, gmixed_out, sums_out,
):
    row_count, seq_length, half_length, width, ff_half, per_up = sizes
    half = width // 2
    gain_one = table[COL_G1 : COL_G1 + 1, :]
    zero = jnp.zeros((1, width), F32)
    sum_gain, sum_shift, sum_out = zero, zero, zero
    for row in range(2 * row_count):
        rows = slice(row * half_length, (row + 1) * half_length)
        swapped = (row + row_count) % (2 * row_count)
        other_rows = slice(swapped * half_length, (swapped + 1) * half_length)
        grad = gh2[rows, :] + (gfirst_own[rows, :].astype(F32) + gfirst_other[other_rows, :].astype(F32))
        normed = normed_one[rows, :]
        sum_gain += jnp.sum(grad * normed, axis=0, keepdims=True)
        sum_shift += jnp.sum(grad, axis=0, keepdims=True)
        scaled = grad * gain_one
        inverse = inverse_one[rows, 0:1]
        grad = inverse * (scaled - mean_of(scaled) - normed * mean_of(scaled * normed))
        if row < row_count:
            gh1_out[rows, :] = grad
        low = grad.astype(BF16)
        gbranch_out[rows, :] = low
        sum_out += jnp.sum(low.astype(F32), axis=0, keepdims=True)
        gmixed_out[row] = (nt_dot(low[:, :half], wo_own[0]) + nt_dot(low[:, half:], wo_own[1])).astype(BF16)
    sums_out[...] = jnp.concatenate([sum_gain, sum_shift, sum_out, jnp.zeros((5, width), F32)], axis=0)


def attend_back_kernel(
    sizes, slope_ref, dmt, gmixed, query, key, value, gq_out, gk_out, gv_out, heads_out,
):
    row_count, seq_length, half_length, width, ff_half, per_up = sizes
    half = width // 2
    lane = iota((1, LANES), 1)
    masks = [ones_where(lane < HEAD_DIM), ones_where(lane >= HEAD_DIM)]
    sums_q = jnp.zeros((1, half), F32)
    sums_v = jnp.zeros((1, half), F32)
    for row in range(2 * row_count):
        for place in range(half // LANES):
            cols = slice(place * LANES, (place + 1) * LANES)
            q_pair, k_pair, v_pair = query[row, :, cols], key[row, :, cols], value[row, :, cols]
            g_pair = gmixed[row, :, cols]
            found = []
            for sub in range(2):
                slope = slope_ref[2 * place + sub]
                scores = nt_dot(k_pair, q_pair * masks[sub]) - slope * dmt[row]
                peak = jnp.max(scores, axis=0, keepdims=True)
                raised = jnp.exp(scores - peak)
                exact = raised * (1.0 / jnp.sum(raised, axis=0, keepdims=True))
                gprobs = nt_dot(v_pair, g_pair * masks[sub])
                mean = jnp.sum(exact * gprobs, axis=0, keepdims=True)
                gscores = (exact * (gprobs - mean)).astype(BF16)
                found.append(
                    (
                        nn_dot(exact.astype(BF16), g_pair),
                        nn_dot(gscores, q_pair),
                        tn_dot(gscores, k_pair) * 0.125,
                    )
                )
            gvalue, gkey, gquery = (
                jnp.where(lane < HEAD_DIM, a, b).astype(BF16) for a, b in zip(found[0], found[1])
            )
            gv_out[row, :, cols] = gvalue
            gk_out[row, :, cols] = gkey
            gq_out[row * half_length : (row + 1) * half_length, cols] = gquery
        sums_q += jnp.sum(gq_out[row * half_length : (row + 1) * half_length, :].astype(F32), axis=0, keepdims=True)
        sums_v += jnp.sum(gv_out[row].astype(F32), axis=0, keepdims=True)
    heads_out[...] = jnp.concatenate([sums_q, sums_v, jnp.zeros((6, half), F32)], axis=0)


def attend_weight_kernel(
    sizes, core_ref, moved, pooled_low, spread, gq, gk, gv, mixed, gbranch, sums_one, sums_two, heads, gbup,
    heads_out, rest_out, send_out,
):
    row_count, seq_length, half_length, width, ff_half, per_up = sizes
    half = width // 2
    core = core_ref[0]
    heads_out[:, :half] = tn_dot(pooled_low[...], gq[...])
    for index, grad in ((1, gk), (2, gv)):
        total = None
        for row in range(2 * row_count):
            term = tn_dot(moved[row], grad[row])
            total = term if total is None else total + term
        heads_out[:, index * half : (index + 1) * half] = total
    per_chip = width // 16
    for chip in range(16):
        rows = slice(chip * per_chip + per_chip // 2, (chip + 1) * per_chip)
        send_out[chip] = heads_out[rows, :].astype(BF16)
    total = None
    for row in range(2 * row_count):
        term = tn_dot(mixed[row], gbranch[row * half_length : (row + 1) * half_length, :])
        total = term if total is None else total + term
    rest_out[:, :width] = total
    mine = [jnp.where(core == 0, sums[:, :half], sums[:, half:]) for sums in (sums_one, sums_two)]
    per_row = half * per_up // ff_half
    which = (iota((8, ff_half), 1) % per_up) // per_row
    high, low = two_parts(jnp.where(iota((8, ff_half), 0) == which, gbup[...], 0.0))
    ups = nt_dot(high, spread[...]) + nt_dot(low, spread[...])
    stacked = jnp.concatenate(
        [
            heads[0:2], mine[0][2:3], mine[0][0:2], mine[1][2:3], mine[1][0:2], ups,
            jnp.zeros((LANES - 16, half), F32),
        ],
        axis=0,
    )
    rest_out[:, width:] = stacked.T


def merge_kernel(core_ref, chip_ref, turn_ref, heads, rest, received, send_one, keep_one, send_two, keep_two):
    core = core_ref[0]
    width = heads.shape[0]
    half = width // 2
    per_row = width // 32
    own = pl.multiple_of(core * half, LANES)
    theirs = pl.multiple_of((1 - core) * half, LANES)
    for m in range(4):
        up, across = divmod(m, 2)
        one, one_at = (send_one, up) if across else (keep_one, up)
        two, two_at = (send_two, across) if up else (keep_two, across)
        for z in range(4):
            chip = 4 * m + turn_ref[z]
            mine = heads[pl.ds(pl.multiple_of(chip * 2 * per_row, 8), per_row), :]
            got = received[chip].astype(F32)
            place = pl.multiple_of(chip_ref[4 * m + z] * per_row, 8)
            outer = rest[pl.ds(place, per_row), :]
            for out, at, index, base in ((one, one_at, 0, 0), (one, one_at, 1, width), (two, two_at, 2, 0)):
                columns = slice(index * half, (index + 1) * half)
                out[at, z, :, pl.ds(base + own, half)] = mine[:, columns].astype(out.dtype)
                out[at, z, :, pl.ds(base + theirs, half)] = got[:, columns].astype(out.dtype)
            one[one_at, z, :, 2 * width :] = outer[:, width:].astype(one.dtype)
            two[two_at, z, :, width:] = outer[:, :width].astype(two.dtype)


def finish_kernel(mine_one, mine_two, first, second, third, q_out, k_out, v_out, o_out, *vectors):
    width = q_out.shape[1]
    per_row = q_out.shape[0]
    split = mine_one.shape[1]

    def total(own, start, size, base):
        terms = [a[:, base + start : base + start + size].astype(F32) for a in (first, second, third)]
        return own[:, start : start + size] + (terms[0] + (terms[1] + terms[2]))

    q_out[...] = total(mine_one, 0, width, 0)
    k_out[...] = total(mine_one, width, width, 0)
    v_out[...] = total(mine_two, 0, width, split)
    o_out[...] = total(mine_two, width, width, split)
    high, low = two_parts(total(mine_one, 2 * width, LANES, 0))
    eye = ones_where(iota((16, LANES), 0) == iota((16, LANES), 1))
    table = nt_dot(eye, high) + nt_dot(eye, low)
    for index in range(8):
        vectors[index][...] = table[index : index + 1, :]
    wide = vectors[8].shape[1]
    high, low = two_parts(table)
    fold = ones_where(iota((per_row, wide), 1) % per_row == iota((per_row, wide), 0))
    spread = nn_dot(high, fold) + nn_dot(low, fold)
    shape = (16, wide)
    picked = jnp.where(iota(shape, 0) == COL_BU + iota(shape, 1) // per_row, spread, 0.0)
    vectors[8][...] = jnp.sum(picked, axis=0, keepdims=True)


def input_grad(sizes, row, gq, gk, gv, wa, perm, extra):
    row_count, seq_length, half_length, width, ff_half, per_up = sizes
    half = width // 2
    grad = nt_dot(gk[row], wa[:, half:width]) + nt_dot(gv[row], wa[:, width:])
    high, low = two_parts(nt_dot(gq[row * half_length : (row + 1) * half_length, :], wa[:, :half]))
    shape = (seq_length, half_length)
    split = jnp.where(iota(shape, 0) // 2 == iota(shape, 1), 0.5, 0.0).astype(BF16)
    grad = grad + (nn_dot(split, high) + nn_dot(split, low))
    if extra is None:
        return nt_dot(grad.astype(BF16), perm[...])
    high, low = two_parts(grad)
    grad = nt_dot(high, perm[...]) + nt_dot(low, perm[...])
    high, low = two_parts(extra)
    return grad + (nn_dot(split, high) + nn_dot(split, low))


def other_inputs_kernel(sizes, gq, gk, gv, wa, perm, send_out):
    row_count, seq_length = sizes[0], sizes[1]
    for local in range(row_count):
        grad = input_grad(sizes, row_count + local, gq, gk, gv, wa, perm, None)
        send_out[local * seq_length : (local + 1) * seq_length, :] = grad.astype(BF16)


def own_inputs_kernel(sizes, gq, gk, gv, wa, perm, gh1, received, grad_out):
    row_count, seq_length, half_length = sizes[0], sizes[1], sizes[2]
    for local in range(row_count):
        extra = gh1[local * half_length : (local + 1) * half_length, :]
        grad = input_grad(sizes, local, gq, gk, gv, wa, perm, extra)
        rows = slice(local * seq_length, (local + 1) * seq_length)
        grad_out[rows, :] = grad + received[rows, :].astype(F32)


def run_kernel(kernel, outs, operands, scratch=(), scalars=0, weight=1, spare=8):
    specs = [pl.BlockSpec(memory_space=pltpu.SMEM)] * scalars
    specs += [pl.BlockSpec(memory_space=pltpu.VMEM)] * (len(operands) - scalars)
    moved = sum(a.size * a.dtype.itemsize for a in list(operands) + list(outs))
    held = sum(math.prod(a.shape) * 4 for a in scratch)
    return pl.pallas_call(
        kernel,
        out_shape=tuple(outs),
        in_specs=specs,
        out_specs=tuple(pl.BlockSpec(memory_space=pltpu.VMEM) for _ in outs),
        scratch_shapes=list(scratch),
        compiler_params=pltpu.CompilerParams(vmem_limit_bytes=int(moved * 1.05) + held + spare * MIB),
        cost_estimate=pl.CostEstimate(flops=int(weight * 1e9), bytes_accessed=int(weight * 1e6), transcendentals=0),
    )(*operands)


def shape_of(shape, dtype):
    return jax.ShapeDtypeStruct(shape, dtype)


def shift(array, step):
    return lax.ppermute(array, "fsdp", [(i, i ^ (4 * step)) for i in range(16)])


def swap(array, bit):
    return lax.ppermute(array, "fsdp", [(i, i ^ bit) for i in range(16)])


def gather_z(pack):
    return [pack] + [shift(pack, step) for step in (1, 2, 3)]


def onward(array, step):
    return lax.ppermute(array, "fsdp", [(i, (i + 4 * step) % 16) for i in range(16)])


def pair_z(pack):
    return jnp.stack([pack, shift(pack, 2)], axis=0)


def column_of(pair, rest, part):
    return jnp.concatenate([pair[0, part], rest[0, part], pair[1, part], rest[1, part]], axis=0)


def near_pieces(one, two):
    return jnp.stack([one, swap(one, 1)], axis=0), jnp.stack([two, swap(two, 2)], axis=0)


def far_pieces(one_near, two_near):
    return swap(one_near, 2), swap(two_near, 1)


def all_pieces(near, far):
    return near[0], far[0], near[1], far[1]


def after(arrays, others):
    return lax.optimization_barrier((arrays, others))[0]


def scatter_near(blocks):
    return swap(blocks[0], 1), swap(blocks[2], 2)


def scatter_far(blocks, got):
    keep_one, keep_two = blocks[1], blocks[3]
    got_one, got_two = got
    next_one = (keep_one[1] + got_one[1].astype(F32)).astype(BF16)
    next_two = (keep_two[1] + got_two[1].astype(F32)).astype(BF16)
    last_one, last_two = swap(next_one, 2), swap(next_two, 1)
    one = keep_one[0] + got_one[0].astype(F32) + last_one.astype(F32)
    two = keep_two[0] + got_two[0].astype(F32) + last_two.astype(F32)
    return one, two


def send_z(parts):
    rows = [a.shape[0] // 4 for a in parts]
    axis = 0 if len({a.shape for a in parts}) == 1 else -1
    received = []
    for step in (1, 2, 3):
        blocks = [a[step * n : (step + 1) * n].astype(BF16) for a, n in zip(parts, rows)]
        received.append(onward(jnp.concatenate(blocks, axis=axis), step))
    return [a[:n] for a, n in zip(parts, rows)], received


def sum_z(mine, received):
    axis = 0 if len({a.shape for a in mine}) == 1 else -1
    ends = [0]
    for block in mine:
        ends.append(ends[-1] + block.shape[axis])
    return [
        block + sum(lax.slice_in_dim(got, start, end, axis=axis).astype(F32) for got in received)
        for block, start, end in zip(mine, ends, ends[1:])
    ]


def half_columns(array, which):
    size = array.shape[1] // 2
    return lax.dynamic_slice_in_dim(array, which * size, size, axis=1)


def halves(array):
    size = array.shape[1] // 2
    return [array[:, :size], array[:, size:]]


def as_pieces(one, two):
    one, two = (a.reshape((4, a.shape[0] // 4) + a.shape[1:]) for a in (one, two))
    return one[:2], one[2:], two[0::2], two[1::2]


def gather_flat(core, weights):
    w_q, w_k, w_v, w_o, biases, w_up, w_down = (lax.all_gather(w, AXES, axis=0, tiled=True) for w in weights)
    width = w_q.shape[0]
    half = width // 2
    wo = jnp.concatenate(halves(lax.dynamic_slice_in_dim(w_o, core * half, half)), axis=0)
    q, k, v = (half_columns(w, core) for w in (w_q, w_k, w_v))
    pieces_a = as_pieces(jnp.concatenate([q, k, biases], axis=1), jnp.concatenate([v, wo], axis=1))
    up = halves(half_columns(w_up, core))
    ff_half = w_down.shape[0] // 2
    down = lax.dynamic_slice_in_dim(w_down, core * ff_half, ff_half).reshape(16, 2, -1, width)
    return pieces_a, as_pieces(*up), as_pieces(*(down[:, part].reshape(-1, width) for part in range(2)))


def scatter_rows(array):
    return lax.psum_scatter(array, AXES, scatter_dimension=0, tiled=True)


def placed(array, core, axis):
    shape = list(array.shape)
    shape[axis] *= 2
    return lax.dynamic_update_slice_in_dim(jnp.zeros(shape, array.dtype), array, core * array.shape[axis], axis)


def whole_of(blocks):
    send_one, keep_one, send_two, keep_two = (a.astype(F32) for a in blocks)
    one = jnp.stack([keep_one, send_one], axis=1)
    two = jnp.stack([keep_two, send_two], axis=0)
    return [a.reshape((-1,) + a.shape[3:]) for a in (one, two)]


def scatter_ffn_flat(core, up_blocks, down_blocks):
    up = placed(jnp.concatenate(whole_of(up_blocks), axis=1), core, 1)
    one, two = whole_of(down_blocks)
    width = one.shape[1]
    down = jnp.stack([one.reshape(16, -1, width), two.reshape(16, -1, width)], axis=1).reshape(-1, width)
    return scatter_rows(up), scatter_rows(placed(down, core, 0))


def scatter_attention_flat(core, heads, rest):
    width = heads.shape[0]
    half = width // 2
    found = [scatter_rows(placed(heads[:, i * half : (i + 1) * half], core, 1)) for i in range(3)]
    return found + [scatter_rows(placed(a, core, 0)) for a in (rest[:, :width], rest[:, width:])]


def body(mesh_shape, *args):
    (
        inputs, segments, w_q, b_q, w_k, w_v, b_v, w_o, b_o, ln1_gain, ln1_bias, w_up, b_up, w_down,
        b_down, ln2_gain, ln2_bias, grad_out,
    ) = args
    dp_size, fsdp_size = mesh_shape
    by_chips = (dp_size, fsdp_size) == (2, 16)
    row_count, seq_length, width = inputs.shape
    half_length = seq_length // 2
    half = width // 2
    per_row, ff = w_up.shape
    ff_half = ff // 2
    per_up = w_down.shape[0]
    ratio = per_up // per_row
    rows2 = 2 * row_count
    tokens = rows2 * half_length
    core = lax.axis_index("dp") & 1
    core_at = core.reshape(1).astype(jnp.int32)
    heads = width // HEAD_DIM
    slopes = 2.0 ** (-8.0 * (jnp.arange(heads, dtype=F32) + 1.0) / heads)
    slopes = jnp.where(core == 0, slopes[: heads // 2], slopes[heads // 2 :])
    swap_pairs = [(i, i ^ 1) for i in range(dp_size)]

    def swap_cores(array):
        return lax.ppermute(array, "dp", swap_pairs)

    place = jnp.arange(width, dtype=jnp.int32)
    if by_chips:
        index = lax.axis_index("fsdp")
        z, yx = index >> 2, index & 3
        m, s = place // (width // 4), place // (width // 16) % 4
        chip = 4 * (z ^ s) + (yx ^ m)
        order = (core ^ (place // per_row % 2)) * half + chip * per_row + place % per_row
        number = jnp.arange(16, dtype=jnp.int32)
        chip_at = 4 * (z ^ (number & 3)) + (yx ^ (number // 4))
        chip_to = 4 * ((z + number) & 3) + (yx ^ (number // 4))
        turn = z ^ ((z + number[:4]) & 3)
        spread_rows = per_up
    else:
        order, chip_at, spread_rows = place, jnp.arange(16, dtype=jnp.int32), per_up
        chip_to, turn = chip_at, chip_at[:4]
    sizes = (row_count, seq_length, half_length, width, ff_half, spread_rows)
    order = jnp.broadcast_to(order, (8, width)).astype(jnp.int32)

    vectors = (b_q, b_v, b_o, ln1_gain, ln1_bias, b_down, ln2_gain, ln2_bias)
    def gathered_rows(hidden, upstream, numbers):
        seg_rows = jnp.pad(numbers.astype(BF16), ((0, 16 - row_count), (0, width - seq_length)))
        own = jnp.concatenate([hidden.reshape(-1, width), upstream.reshape(-1, width), seg_rows], axis=0)
        return own, swap_cores(own)

    def prepare(acts):
        return run_kernel(
            functools.partial(ready_kernel, sizes),
            [
                shape_of((width, width), BF16),
                shape_of((rows2, seq_length, width), BF16),
                shape_of((tokens, width), F32),
                shape_of((tokens, width), BF16),
                shape_of((rows2, half_length, seq_length), F32),
                shape_of((rows2, seq_length, half_length), F32),
                shape_of((half, ff_half), BF16),
            ],
            [order, *acts],
            weight=20,
        )

    if by_chips:
        base = width + LANES + half
        send, own, own_up = run_kernel(
            pack_kernel,
            [shape_of((per_row, base + ff_half), BF16), shape_of((per_row, base), BF16), shape_of((per_row, ff_half), BF16)],
            [core_at, w_q, w_k, w_v, w_up, b_up.reshape(1, -1)] + [v.reshape(1, -1) for v in vectors],
            scalars=1,
            spare=54,
        )
        received = swap_cores(send)
        act_own, act_other = gathered_rows(*after((inputs, grad_out, segments), received))
        pack_a, pack_up = run_kernel(
            chip_pack_kernel,
            [shape_of((2, per_row, base + half), BF16), shape_of((2, 2, per_row, width), BF16)],
            [core_at, own, received, own_up, w_o],
            scalars=1,
            spare=54,
        )
        pack_up = pack_up.reshape(2, 2 * per_row, width)
        pack_down = w_down.reshape(2, 2 * per_row, width)
        around = gather_z(after(pack_a, act_other).reshape(2 * per_row, base + half))
        split = width + LANES
        one = jnp.concatenate([a[:, :split] for a in around], axis=0)
        two = jnp.concatenate([a[:, split:] for a in around], axis=0)
        near_a = near_pieces(one, two)
        up_pair = pair_z(after(pack_up, (one, two)))
        far_a = far_pieces(*near_a)
        up_pair = after(up_pair, near_a)
        up_rest = shift(up_pair, 1)
        down_pair = pair_z(after(pack_down, up_pair))
        perm, *prepared = prepare(after((act_own, act_other), (near_a, up_pair)))
        up_pair, up_rest = after((up_pair, up_rest), (perm, far_a))
        ups = [column_of(up_pair, up_rest, part) for part in range(2)]
        near_up = near_pieces(*ups)
        pieces_a = all_pieces(near_a, after(far_a, ups))
        down_pair = after(down_pair, ups)
        down_rest = shift(down_pair, 1)
    else:
        act_own, act_other = gathered_rows(inputs, grad_out, segments)
        biases = jnp.stack(vectors, axis=0)
        biases = jnp.concatenate([biases, b_up.reshape(ratio, per_row)], axis=0)
        biases = jnp.pad(biases, ((0, LANES - 8 - ratio), (0, 0))).T
        perm, *prepared = prepare((act_own, act_other))
        near_up, (pieces_a, pieces_up, pieces_down) = (), gather_flat(core, (w_q, w_k, w_v, w_o, biases, w_up, w_down))
    moved, pooled, pooled_low, dm, dmt, spread = prepared
    q_rows, k_rows, v_rows, wa, wo_own, table, bup = run_kernel(
        functools.partial(project_kernel, sizes),
        [
            shape_of((rows2, half_length, half), BF16),
            shape_of((rows2, seq_length, half), BF16),
            shape_of((rows2, seq_length, half), BF16),
            shape_of((width, 3 * half), BF16),
            shape_of((2, half, half), BF16),
            shape_of((16, width), F32),
            shape_of((8, ff_half), F32),
        ],
        [core_at, moved, pooled_low, perm, spread, *pieces_a],
        [pltpu.VMEM((width, half), BF16), pltpu.VMEM((width, LANES), BF16)],
        scalars=1,
    )
    if by_chips:
        near_up = after(near_up, q_rows)
        downs = [column_of(*after((down_pair, down_rest), near_up), part) for part in range(2)]
        near_down = near_pieces(*downs)
        pieces_up = all_pieces(near_up, far_pieces(*near_up))
        pieces_down = all_pieces(near_down, far_pieces(*near_down))
        q_rows = after(q_rows, near_down)
    (mixed,) = run_kernel(
        functools.partial(attend_kernel, sizes),
        [shape_of((rows2, half_length, half), BF16)],
        [slopes, dm, q_rows, k_rows, v_rows],
        scalars=1,
    )
    wo_other = swap_cores(wo_own)
    mixed_other = swap_cores(mixed)
    normed_one, inverse_one, first_low, active, bend, up = run_kernel(
        functools.partial(ffn_up_kernel, sizes),
        [
            shape_of((tokens, width), F32),
            shape_of((tokens, LANES), F32),
            shape_of((tokens, width), BF16),
            shape_of((tokens, ff_half), BF16),
            shape_of((tokens, ff_half), F32),
            shape_of((2, width, width), BF16),
        ],
        [pooled, mixed, mixed_other, wo_own, wo_other, table, bup, perm, *pieces_up],
    )
    part_two, down = run_kernel(
        functools.partial(ffn_down_kernel, sizes),
        [shape_of((tokens, width), BF16), shape_of((ff_half, width), BF16)],
        [chip_at, active, *pieces_down],
        scalars=1,
    )
    part_other = swap_cores(part_two)
    block = width // 4
    send_shape, keep_shape = shape_of((2, block, width), BF16), shape_of((2, block, width), F32)
    output, gh2, gsec, sums_two, *down_blocks = run_kernel(
        functools.partial(second_norm_kernel, sizes),
        [
            shape_of((row_count * half_length, width), BF16),
            shape_of((tokens, width), F32),
            shape_of((tokens, width), BF16),
            shape_of((8, width), F32),
            send_shape, keep_shape, send_shape, keep_shape,
        ],
        [chip_to, act_own, act_other, normed_one, part_two, part_other, table, active],
        [pltpu.VMEM((ff_half, width), F32)],
        scalars=1,
    )
    ginner, gfirst, gbup = run_kernel(
        functools.partial(ffn_back_kernel, sizes),
        [shape_of((tokens, ff_half), BF16), shape_of((tokens, width), BF16), shape_of((8, ff_half), F32)],
        [gsec, bend, perm, up, down],
    )
    gfirst_other = swap_cores(gfirst)
    up_blocks = run_kernel(
        ffn_weight_kernel,
        [send_shape, keep_shape, send_shape, keep_shape],
        [turn, first_low, ginner],
        [pltpu.VMEM((width, width), F32)],
        scalars=1,
    )
    gh1, gbranch, gmixed, sums_one = run_kernel(
        functools.partial(first_norm_kernel, sizes),
        [
            shape_of((row_count * half_length, width), F32),
            shape_of((tokens, width), BF16),
            shape_of((rows2, half_length, half), BF16),
            shape_of((8, width), F32),
        ],
        [normed_one, inverse_one, gh2, gfirst, after(gfirst_other, tuple(up_blocks)), table, wo_own],
    )
    gq, gk, gv, head_sums = run_kernel(
        functools.partial(attend_back_kernel, sizes),
        [
            shape_of((tokens, half), BF16),
            shape_of((rows2, seq_length, half), BF16),
            shape_of((rows2, seq_length, half), BF16),
            shape_of((8, half), F32),
        ],
        [slopes, dmt, gmixed, q_rows, k_rows, v_rows],
        scalars=1,
    )
    grad_heads, grad_rest, heads_send = run_kernel(
        functools.partial(attend_weight_kernel, sizes),
        [
            shape_of((width, 3 * half), F32),
            shape_of((half, width + LANES), F32),
            shape_of((16, width // 32, 3 * half), BF16),
        ],
        [core_at, moved, pooled_low, spread, gq, gk, gv, mixed, gbranch, sums_one, sums_two, head_sums, gbup],
        scalars=1,
    )
    if by_chips:
        down_parts = scatter_far(down_blocks, after(scatter_near(down_blocks), gq))
        heads_other = swap_cores(heads_send)
        got_up = after(scatter_near(up_blocks), heads_send)
        grad_heads = after(grad_heads, got_up)
        blocks = (4, per_row)
        columns_one, columns_two = 2 * width + LANES, 2 * width
        attend_blocks = run_kernel(
            merge_kernel,
            [
                shape_of((2,) + blocks + (columns_one,), BF16),
                shape_of((2,) + blocks + (columns_one,), F32),
                shape_of((2,) + blocks + (columns_two,), BF16),
                shape_of((2,) + blocks + (columns_two,), F32),
            ],
            [core_at, chip_to, turn, grad_heads, grad_rest, heads_other],
            scalars=3,
        )
        attend_blocks = after(tuple(attend_blocks), down_parts)
        up_parts = scatter_far(up_blocks, got_up)
        got_attend = scatter_near(attend_blocks)
        gq = after(gq, up_parts)
    (inputs_send,) = run_kernel(
        functools.partial(other_inputs_kernel, sizes),
        [shape_of((row_count * seq_length, width), BF16)],
        [gq, gk, gv, wa, perm],
    )
    if by_chips:
        parts_f, z_blocks = send_z([*down_parts, *up_parts])
        parts_a = scatter_far(attend_blocks, got_attend)
        inputs_send = after(inputs_send, parts_a)
    inputs_other = swap_cores(inputs_send)
    (grad_inputs,) = run_kernel(
        functools.partial(own_inputs_kernel, sizes),
        [shape_of((row_count * seq_length, width), F32)],
        [gq, gk, gv, wa, perm, gh1, inputs_other],
    )
    if by_chips:
        z_blocks = after(z_blocks, parts_a)
        down_one, down_two, up_one, up_two = sum_z(parts_f, z_blocks)
        grad_down = jnp.concatenate([down_one, down_two], axis=0)
        up_got = swap_cores(jnp.concatenate([up_one[per_row:], up_two[per_row:]], axis=1))
        up_mine = jnp.concatenate([up_one[:per_row], up_two[:per_row]], axis=1)
        grad_up = jnp.where(
            core == 0, jnp.concatenate([up_mine, up_got], -1), jnp.concatenate([up_got, up_mine], -1)
        )
        mine, received = send_z(list(parts_a))
        received = after(received, (grad_inputs, grad_up, grad_down))
        square, vector = shape_of((per_row, width), F32), shape_of((1, per_row), F32)
        found = run_kernel(
            finish_kernel,
            [square] * 4 + [vector] * 8 + [shape_of((1, per_up), F32)],
            [a.reshape(per_row, -1) for a in (*mine, *received)],
        )
        grad_q, grad_k, grad_v, grad_o = found[:4]
        g_bq, g_bv, g_bo, g_g1, g_s1, g_bd, g_g2, g_s2, g_bu = (a.reshape(-1) for a in found[4:])
    else:
        grad_up, grad_down = scatter_ffn_flat(core, up_blocks, down_blocks)
        found = scatter_attention_flat(core, grad_heads, grad_rest)
        grad_q, grad_k, grad_v, grad_o = found[:4]
        small = found[4].T
        g_bq, g_bv, g_bo, g_g1, g_s1, g_bd, g_g2, g_s2 = (small[i] for i in range(8))
        g_bu = small[8 : 8 + ratio].reshape(per_up)
    return (
        output.reshape(row_count, half_length, width),
        grad_inputs.reshape(row_count, seq_length, width),
        grad_q, g_bq, grad_k, grad_v, g_bv, grad_o, g_bo, g_g1, g_s1, grad_up, g_bu, grad_down, g_bd, g_g2, g_s2,
    )


def solution(mesh):
    rows, matrix, vector = P(AXES, None, None), P(AXES, None), P(AXES)
    in_specs = (
        rows, matrix, matrix, vector, matrix, matrix, vector, matrix, vector, vector, vector, matrix, vector,
        matrix, vector, vector, vector, rows,
    )
    out_specs = (
        rows, rows, matrix, vector, matrix, matrix, vector, matrix, vector, vector, vector, matrix, vector,
        matrix, vector, vector, vector,
    )
    shape = (mesh.shape["dp"], mesh.shape["fsdp"])
    return jax.shard_map(
        functools.partial(body, shape), mesh=mesh, in_specs=in_specs, out_specs=out_specs, check_vma=False
    )
```
